128 devices in a mesh: owner: 32 (over z, y, core), col: 4 (over x).
Axes of the slice: x: 4, y: 4, z: 4, core: 2. Of those that a mesh axis runs over, the one named last changes fastest.
Arguments:
- pooled_grad: bfloat16 [32768, 32, 512], P('owner', None, 'col'), may hold values from -40 to 40
- segment_map: int32 [32768, 32, 4], P('owner'), may hold values from 0 to 1023, as said below
- unique_rows: int32 [32, 1024], P('owner'), may hold values from 0 to 8191, as said below
- live_counts: int32 [32], P('owner'), may hold values from 512 to 1024
- embedding: float32 [32, 8192, 512], P('owner', None, 'col'), may hold values from -6 to 6
- accumulator: float32 [32, 8192], P('owner'), may hold values from 50 to 5000
Outputs:
- new_embedding: float32 [32, 8192, 512], P('owner', None, 'col')
- new_accumulator: float32 [32, 8192], P('owner')
The draws below stay inside these ranges and needn't reach their ends.
Inputs may be any that keep to these rules, and one draw needn't show every extreme that they name: `segment_map`: every entry for table t is below live_counts[t]. `unique_rows`: the slots of table t below live_counts[t] hold distinct rows; later slots hold rows of the table and are ignored.
All inputs are finite; a program needn't handle non-finite values.
Results may differ from the reference program's by a relative error of at most 0.002.
Values may be sent and summed in bfloat16 or wider, within the bound.
No kernel may reach another device: no remote copies, remote signals or barrier semaphores. Data moves between devices by JAX's collectives and lax.ppermute only.
A program may use at most 128 MiB of HBM per device.

```python
import math
import jax
import jax.numpy as jnp
from jax import lax

E = 512
HOT = 4
UNIQ = 1024
VOCAB = 8192
TABLES = 32
BATCH = 32768


def shared_counts(key):
    first_key = jax.random.fold_in(key, 11)
    second_key = jax.random.fold_in(key, 12)
    counts_drawn = jax.random.randint(first_key, (TABLES,), UNIQ // 2, UNIQ + 1)
    full_table = jax.random.randint(second_key, (), 0, TABLES)
    counts_drawn = jnp.where(jnp.arange(TABLES) == full_table, UNIQ, counts_drawn)
    return counts_drawn.astype(jnp.int32)


def draw_live_counts(key, part):
    counts_drawn = shared_counts(key)
    return counts_drawn


def draw_segment_map(key, part):
    counts_drawn = shared_counts(key)
    key = jax.random.fold_in(key, 4)
    slots_drawn = jax.random.randint(key, (BATCH, TABLES, HOT), 0, counts_drawn[None, :, None])
    slots_drawn = slots_drawn.at[0, :, 0].set(counts_drawn - 1)
    return slots_drawn.astype(jnp.int32)


def table_rows(single):
    inner_key = jax.random.fold_in(single, 1)
    order_key = jax.random.fold_in(single, 2)
    middle = jax.random.permutation(inner_key, VOCAB - 2)[:UNIQ - 2] + 1
    chosen = jnp.concatenate([jnp.array([0, VOCAB - 1], dtype=jnp.int32), middle.astype(jnp.int32)])
    return chosen[jax.random.permutation(order_key, UNIQ)]


def draw_unique_rows(key, part):
    counts_drawn = shared_counts(key)
    key = jax.random.fold_in(key, 5)
    table_keys = jax.random.split(key, TABLES)
    live_rows = jax.vmap(table_rows)(table_keys).astype(jnp.int32)
    picked = jax.random.randint(jax.random.fold_in(key, 6), (TABLES, UNIQ), 0, counts_drawn[:, None])
    repeated = jnp.take_along_axis(live_rows, picked, axis=1)
    position = jnp.arange(UNIQ)[None, :]
    return jnp.where(position < counts_drawn[:, None], live_rows, repeated).astype(jnp.int32)


def draw_pooled_grad(key, part):
    key = jax.random.fold_in(key, 7)
    first_key, second_key = jax.random.split(key)
    column_scale = 0.3 * 10.0 ** (jnp.arange(E, dtype=jnp.float32) / E)
    values = jax.random.normal(first_key, (BATCH, TABLES, E), jnp.float32)
    scales = jnp.exp(jax.random.uniform(second_key, (BATCH, TABLES, 1), jnp.float32, math.log(0.5), math.log(5.0)))
    return jnp.clip(values * scales * column_scale, -40.0, 40.0).astype(jnp.bfloat16)


def levels(rng, dims, cuts, least, largest):
    def one(axis_at, parts):
        heights = jax.random.uniform(jax.random.fold_in(jax.random.fold_in(rng, 6), axis_at), (parts,), jnp.float32, least / len(cuts), largest / len(cuts))
        return jnp.repeat(jnp.exp(heights), dims[axis_at] // parts).reshape((-1,) + (1,) * (len(dims) - axis_at - 1))

    gain = one(*cuts[0])
    for cut in cuts[1:]:
        gain = gain * one(*cut)
    return gain


def bell_draw(own_key, shape, scale, limit, shards=(), kind=jnp.bfloat16):
    level = levels(own_key, shape, shards, -0.22, 0.18) if shards else 1.0
    values = jax.random.normal(own_key, shape, jnp.float32) * scale * level
    return jnp.minimum(jnp.maximum(values, -limit), limit).astype(kind)


def setup_inputs(seed: int = 0) -> dict:
    splits = jax.random.split(jax.random.key(seed), 7)
    pooled_grad = draw_pooled_grad(jax.random.fold_in(splits[6], 71), 0)
    segment_map = draw_segment_map(jax.random.fold_in(splits[6], 71), 0)
    unique_rows = draw_unique_rows(jax.random.fold_in(splits[6], 71), 0)
    live_counts = draw_live_counts(jax.random.fold_in(splits[6], 71), 0)
    embedding = bell_draw(splits[4], (TABLES, VOCAB, E), 1.0, 6.0, ((0, 32), (2, 4)), jnp.float32)
    accumulator = jnp.clip(jnp.exp(math.log(5000.0) - 4.6051702 * jax.random.uniform(splits[5], (TABLES, VOCAB), jnp.float32) ** levels(splits[5], (TABLES, VOCAB), ((0, 32),), -0.2, 0.2)), 50.0, 5000.0)
    return dict(pooled_grad=pooled_grad, segment_map=segment_map, unique_rows=unique_rows, live_counts=live_counts, embedding=embedding, accumulator=accumulator)


learn_rate = 0.5
epsilon = 1e-08

def table_update(pooled_rows, segment_rows, slot_rows, live_total, weights, accum_rows):
    hot_count = segment_rows.shape[1]
    widths = pooled_rows.shape[1]
    spread = jnp.broadcast_to(pooled_rows.astype(jnp.float32)[:, None, :], (pooled_rows.shape[0], hot_count, widths))
    gradient = jax.ops.segment_sum(spread.reshape(-1, widths), segment_rows.reshape(-1), num_segments=UNIQ)
    mean_square = lax.optimization_barrier(jnp.sum(gradient * gradient, axis=1)) / E
    new_acc = accum_rows[slot_rows] + mean_square
    new_rows = weights[slot_rows] - learn_rate * gradient / (jnp.sqrt(new_acc)[:, None] + epsilon)
    live = jnp.arange(UNIQ, dtype=jnp.int32) < live_total
    target = jnp.where(live, slot_rows, VOCAB).astype(jnp.int32)
    return (weights.at[target].set(new_rows, mode='drop'), accum_rows.at[target].set(new_acc, mode='drop'))

def one_table(packed):
    return table_update(packed[0], packed[1], packed[2], packed[3], packed[4], packed[5])

def reference(pooled_grad, segment_map, unique_rows, live_counts, embedding, accumulator):
    new_embedding, new_accumulator = lax.map(one_table, (jnp.moveaxis(pooled_grad, 1, 0), jnp.moveaxis(segment_map, 1, 0), unique_rows, live_counts, embedding, accumulator))
    return (new_embedding, new_accumulator)
```

```python
import functools

import jax
import jax.numpy as jnp
from jax import lax
from jax.experimental import pallas as pl
from jax.experimental.pallas import tpu as pltpu
from jax.sharding import Mesh
from jax.sharding import PartitionSpec as P

learn_rate = 0.5
epsilon = 1e-08
MIB = 2**20
BF = jnp.bfloat16
F32 = jnp.float32
VMEM = pl.BlockSpec(memory_space=pltpu.VMEM)
SMEM = pl.BlockSpec(memory_space=pltpu.SMEM)
ANY = pl.BlockSpec(memory_space=pl.ANY)


def prep_body(x_ref, seg_ref, o_ref, ids_ref):
    o_ref[...] = jnp.swapaxes(x_ref[...], 0, 1)
    seg = [seg_ref[:, h, :] for h in range(4)]
    same = lambda a, b: jnp.where(seg[a] == seg[b], 1, 0)
    e01, e02, e03 = same(0, 1), same(0, 2), same(0, 3)
    e12, e13, e23 = same(1, 2), same(1, 3), same(2, 3)
    rows = [
        seg[0],
        jnp.where(e01 > 0, -1, seg[1]),
        jnp.where(e02 + e12 > 0, -1, seg[2]),
        jnp.where(e03 + e13 + e23 > 0, -1, seg[3]),
        1 + e01 + e02 + e03,
        1 + e12 + e13,
        1 + e23,
        jnp.ones_like(e01),
    ]
    for r, value in enumerate(rows):
        ids_ref[:, r, :] = value.astype(F32)


def prep(pooled, seg):
    batch, tables, columns = pooled.shape
    block = 128
    return pl.pallas_call(
        prep_body,
        grid=(batch // block,),
        in_specs=[
            pl.BlockSpec((block, tables, columns), lambda i: (i, 0, 0)),
            pl.BlockSpec((tables, 4, block), lambda i: (0, 0, i)),
        ],
        out_specs=[
            pl.BlockSpec((tables, block, columns), lambda i: (0, i, 0)),
            pl.BlockSpec((tables, 8, block), lambda i: (0, 0, i)),
        ],
        out_shape=[
            jax.ShapeDtypeStruct((tables, batch, columns), BF),
            jax.ShapeDtypeStruct((tables, 8, batch), F32),
        ],
        compiler_params=pltpu.CompilerParams(vmem_limit_bytes=40 * MIB),
        name="prep",
    )(pooled, seg)


def tile_sum(ids, weights, x, first, rows):
    batch = x.shape[0]
    number = lax.broadcasted_iota(jnp.int32, (rows, batch), 0).astype(F32).astype(BF)
    local = (ids - float(first)).astype(BF)
    hit = jnp.zeros((rows, batch), BF)
    for h in range(3, -1, -1):
        here = number == jnp.broadcast_to(local[h : h + 1], (rows, batch))
        hit = jnp.where(here, jnp.broadcast_to(weights[4 + h : 5 + h], (rows, batch)), hit)
    return jnp.dot(hit, x, preferred_element_type=F32)


def sums_body(own, first, splits, core_ref, bound_ref, ids_ref, x_ref, *refs):
    add_refs, out_ref = refs[: len(splits)], refs[-1]
    core = core_ref[0]
    side = core if own else 1 - core
    _, slots, columns = out_ref.shape
    half = slots // 2

    def table_sums(k, add):
        table = 2 * (first + k) + side

        def put(at, rows, value):
            here = pl.ds(at, rows)
            if add is not None:
                value = value + add_refs[add][k - splits[add], here, :].astype(F32)
            out_ref[k, here, :] = value.astype(BF)

        tiles = jnp.clip((bound_ref[table] - half) // 128 + 1, 0, half // 128)
        for n in range(half // 128 + 1):

            @pl.when(tiles == n)
            def _(n=n):
                ids = ids_ref[table]
                weights = ids.astype(BF)
                x = x_ref[table]
                at, end = 0, half + n * 128
                while at < end:
                    rows = min(256, end - at)
                    put(at, rows, tile_sum(ids, weights, x, at, rows))
                    at += rows
                while at < slots:
                    put(at, 128, jnp.zeros((128, columns), F32))
                    at += 128

    starts = list(splits) if splits else [0]
    ends = starts[1:] + [out_ref.shape[0]]
    for add, (begin, end) in enumerate(zip(starts, ends)):

        def step(k, carry, add=add):
            table_sums(k, add if splits else None)
            return carry

        lax.fori_loop(begin, end, step, 0)


def sums(name, core, bound, ids, xt, own, first, count, slots, adds=(), after=()):
    columns = xt.shape[2]
    splits, at = [], 0
    for add in adds:
        splits.append(at)
        at += add.shape[0]
    return pl.pallas_call(
        functools.partial(sums_body, own, first, tuple(splits)),
        in_specs=[SMEM, SMEM, VMEM, VMEM] + [VMEM] * len(adds) + [ANY] * len(after),
        out_specs=VMEM,
        out_shape=jax.ShapeDtypeStruct((count, slots, columns), BF),
        compiler_params=pltpu.CompilerParams(vmem_limit_bytes=12 * MIB),
        name=name,
    )(core, bound, ids, xt, *adds, *after)


def total_body(got_ref, grad_ref, square_ref):
    total = got_ref[0].astype(F32)
    for i in range(1, got_ref.shape[0]):
        total = total + got_ref[i].astype(F32)
    grad_ref[...] = total
    square_ref[...] = jnp.sum((total * total).T, axis=0, keepdims=True)


def total(name, got):
    _, count, columns = got.shape
    return pl.pallas_call(
        total_body,
        in_specs=[VMEM],
        out_specs=[VMEM, VMEM],
        out_shape=[
            jax.ShapeDtypeStruct((count, columns), F32),
            jax.ShapeDtypeStruct((1, count), F32),
        ],
        compiler_params=pltpu.CompilerParams(vmem_limit_bytes=8 * MIB),
        name=name,
    )(got)


def old_body(row_ref, emb_ref, acc_ref, after_ref, old_ref, old_acc_ref):
    def step(i, carry):
        for j in range(8):
            u = i * 8 + j
            row = row_ref[0, u]
            old_ref[pl.ds(u, 1), :] = emb_ref[pl.ds(row, 1), :]
            old_acc_ref[0, u] = acc_ref[0, row]
        return carry

    lax.fori_loop(0, old_ref.shape[0] // 8, step, 0)


def old_values(rows, embedding, accumulator, after):
    slots, columns = rows.shape[1], embedding.shape[1]
    return pl.pallas_call(
        old_body,
        in_specs=[SMEM, VMEM, SMEM, ANY],
        out_specs=[VMEM, SMEM],
        out_shape=[
            jax.ShapeDtypeStruct((slots, columns), F32),
            jax.ShapeDtypeStruct((1, slots), F32),
        ],
        compiler_params=pltpu.CompilerParams(vmem_limit_bytes=12 * MIB),
        name="old_values",
    )(rows, embedding, accumulator, after)


def apply_body(
    width, row_ref, live_ref, emb_in, grad_ref, old_ref, square_ref, old_acc_ref, acc_in,
    emb_out, acc_out, emb_ref, new_ref, new_acc_ref, new_acc_smem, acc_smem, sems,
):
    load = pltpu.make_async_copy(acc_in, acc_smem, sems.at[0])
    load.start()
    fetch = pltpu.make_async_copy(emb_in, emb_ref, sems.at[2])
    fetch.start()
    slots, columns = old_ref.shape
    mean_square = jnp.sum(square_ref[...], axis=0) / width
    new_acc = old_acc_ref[...] + mean_square
    new_acc_ref[...] = new_acc
    move = pltpu.make_async_copy(new_acc_ref, new_acc_smem, sems.at[1])
    move.start()
    scale = learn_rate / (jnp.sqrt(new_acc) + epsilon)
    scale = jnp.broadcast_to(scale, (columns, slots)).T
    new_ref[...] = old_ref[...] - grad_ref[...] * scale
    live = live_ref[0]
    fetch.wait()

    def step(i, carry):
        for j in range(8):
            u = jnp.minimum(i * 8 + j, live - 1)
            emb_ref[pl.ds(row_ref[0, u], 1), :] = new_ref[pl.ds(u, 1), :]
        return carry

    lax.fori_loop(0, (live + 7) // 8, step, 0)
    load.wait()
    move.wait()
    write = pltpu.make_async_copy(emb_ref, emb_out, sems.at[2])
    write.start()

    def acc_step(i, carry):
        for j in range(8):
            u = jnp.minimum(i * 8 + j, live - 1)
            acc_smem[0, row_ref[0, u]] = new_acc_smem[0, u]
        return carry

    lax.fori_loop(0, (live + 7) // 8, acc_step, 0)
    store = pltpu.make_async_copy(acc_smem, acc_out, sems.at[0])
    store.start()
    store.wait()
    write.wait()


def apply_rows(width, rows, live, embedding, gradient, old, squares, old_acc, accumulator):
    slots = rows.shape[1]
    return pl.pallas_call(
        functools.partial(apply_body, width),
        in_specs=[SMEM, SMEM, ANY, VMEM, VMEM, VMEM, VMEM, ANY],
        out_specs=[ANY, ANY],
        out_shape=[
            jax.ShapeDtypeStruct(embedding.shape, F32),
            jax.ShapeDtypeStruct(accumulator.shape, F32),
        ],
        scratch_shapes=[
            pltpu.VMEM(embedding.shape, F32),
            pltpu.VMEM(old.shape, F32),
            pltpu.VMEM((1, slots), F32),
            pltpu.SMEM((1, slots), F32),
            pltpu.SMEM(accumulator.shape, F32),
            pltpu.SemaphoreType.DMA((3,)),
        ],
        compiler_params=pltpu.CompilerParams(vmem_limit_bytes=16 * MIB),
        name="apply_rows",
    )(rows, live, embedding, gradient, old, squares, old_acc, accumulator)


def per_device(pooled_grad, segment_map, unique_rows, live_counts, embedding, accumulator):
    columns = pooled_grad.shape[2]
    slots = unique_rows.shape[1]
    cols = lax.axis_size("col")
    half = slots // 2
    core = lax.axis_index("core").astype(jnp.int32).reshape(1)
    seg = jnp.transpose(segment_map, (1, 2, 0))
    bound = jnp.max(seg, axis=(1, 2))
    xt, ids = prep(pooled_grad, seg)
    swap = lambda a: lax.ppermute(a, "core", [(0, 1), (1, 0)])
    spread = lambda a: lax.all_to_all(a, ("z", "y"), 0, 0, tiled=True)

    chips = xt.shape[0] // 2
    late = chips // 4
    sib_a = sums("sib_a", core, bound, ids, xt, False, 0, chips - late, slots)
    got_a = swap(sib_a)
    sib_b = sums("sib_b", core, bound, ids, xt, False, chips - late, late, slots, (), (sib_a,))
    got_b = swap(sib_b)
    old, old_acc = old_values(unique_rows, embedding[0], accumulator, sib_b)
    own = sums("own", core, bound, ids, xt, True, 0, chips, slots, (got_a, got_b), (old,))
    gradient, squares = total("total", spread(own))
    squares = lax.all_to_all(jnp.broadcast_to(squares[None], (cols, 1, slots)), "col", 0, 0, tiled=True)
    new_embedding, new_accumulator = apply_rows(
        columns * cols, unique_rows, live_counts, embedding[0], gradient, old, squares, old_acc, accumulator
    )
    return (new_embedding[None], new_accumulator)


def solution(mesh):
    owner = ("z", "y", "core")
    split = Mesh(mesh.devices.reshape(4, 4, 2, mesh.devices.shape[1]), owner + ("col",))
    return jax.shard_map(
        per_device,
        mesh=split,
        in_specs=(
            P(owner, None, "col"),
            P(owner, None, None),
            P(owner, None),
            P(owner),
            P(owner, None, "col"),
            P(owner, None),
        ),
        out_specs=(P(owner, None, "col"), P(owner, None)),
        check_vma=False,
    )
```

```python
import functools

import jax
import jax.numpy as jnp
from jax import lax
from jax.experimental import pallas as pl
from jax.experimental.pallas import tpu as pltpu
from jax.sharding import Mesh
from jax.sharding import PartitionSpec as P

learn_rate = 0.5
epsilon = 1e-08
MIB = 2**20
BF = jnp.bfloat16
F32 = jnp.float32
VMEM = pl.BlockSpec(memory_space=pltpu.VMEM)
SMEM = pl.BlockSpec(memory_space=pltpu.SMEM)
ANY = pl.BlockSpec(memory_space=pl.ANY)
COST = pl.CostEstimate(flops=1000, transcendentals=0, bytes_accessed=1000)


def prep_body(x_hbm, seg_hbm, o_ref, ids_ref, bound_ref, x_ref, seg_ref, sems):
    batch = x_ref.shape[0]
    block = 128
    blocks = batch // block
    seg_copy = pltpu.make_async_copy(seg_hbm, seg_ref, sems.at[blocks])
    seg_copy.start()
    copies = []
    for i in range(blocks):
        here = pl.ds(i * block, block)
        copies.append(pltpu.make_async_copy(x_hbm.at[here], x_ref.at[here], sems.at[i]))
        copies[-1].start()
    seg_copy.wait()
    for t in range(seg_ref.shape[0]):
        bound_ref[t] = jnp.max(seg_ref[t])
    seg = [seg_ref[:, h, :] for h in range(4)]
    same = lambda a, b: jnp.where(seg[a] == seg[b], 1, 0)
    e01, e02, e03 = same(0, 1), same(0, 2), same(0, 3)
    e12, e13, e23 = same(1, 2), same(1, 3), same(2, 3)
    rows = [
        seg[0],
        jnp.where(e01 > 0, -1, seg[1]),
        jnp.where(e02 + e12 > 0, -1, seg[2]),
        jnp.where(e03 + e13 + e23 > 0, -1, seg[3]),
        1 + e01 + e02 + e03,
        1 + e12 + e13,
        1 + e23,
        jnp.ones_like(e01),
    ]
    for r, value in enumerate(rows):
        ids_ref[:, r, :] = value.astype(F32)
    for i in range(blocks):
        here = pl.ds(i * block, block)
        copies[i].wait()
        o_ref[:, here, :] = jnp.swapaxes(x_ref[here], 0, 1)


def prep(pooled, seg):
    batch, tables, columns = pooled.shape
    return pl.pallas_call(
        prep_body,
        in_specs=[ANY, ANY],
        out_specs=[VMEM, VMEM, SMEM],
        out_shape=[
            jax.ShapeDtypeStruct((tables, batch, columns), BF),
            jax.ShapeDtypeStruct((tables, 8, batch), F32),
            jax.ShapeDtypeStruct((tables,), jnp.int32),
        ],
        scratch_shapes=[
            pltpu.VMEM(pooled.shape, BF),
            pltpu.VMEM(seg.shape, jnp.int32),
            pltpu.SemaphoreType.DMA((batch // 128 + 1,)),
        ],
        compiler_params=pltpu.CompilerParams(vmem_limit_bytes=40 * MIB),
        cost_estimate=COST,
        name="prep",
    )(pooled, seg)


def tile_sum(ids, weights, x, first, rows):
    batch = x.shape[0]
    number = lax.broadcasted_iota(jnp.int32, (rows, batch), 0).astype(F32).astype(BF)
    local = (ids - first).astype(BF)
    hit = jnp.zeros((rows, batch), BF)
    for h in range(3, -1, -1):
        here = number == jnp.broadcast_to(local[h : h + 1], (rows, batch))
        hit = jnp.where(here, jnp.broadcast_to(weights[4 + h : 5 + h], (rows, batch)), hit)
    return jnp.dot(hit, x, preferred_element_type=F32)


def ring_pos(half):
    at_z, at_y = lax.axis_index("z"), lax.axis_index("y")
    return jnp.where(half == 0, at_z, at_y), jnp.where(half == 0, at_y, at_z)


def half_sums(own, step, add_ref, extra_ref, out_ref, bound_ref, ids_ref, x_ref):
    core = lax.axis_index("core")
    half = core if own else 1 - core
    place = lax.rem(ring_pos(half)[0] + step, 4)
    _, slots, columns = out_ref.shape
    tile = slots // 2

    def put(m, at, value):
        here = pl.ds(at, tile)
        if add_ref is not None:
            value = value + add_ref[m, here, :].astype(F32)
        if extra_ref is not None:
            value = value + extra_ref[m, here, :].astype(F32)
        out_ref[m, here, :] = value.astype(out_ref.dtype)

    def chip_sums(j, carry):
        chip = jnp.where(half == 0, place * 4 + j, j * 4 + place)
        later = [slots + lax.rem(half + c, 2) * tile for c in range(2)]
        filled = [bound_ref[2 * chip + c] >= later[c] for c in range(2)]
        for case in range(4):
            wanted = [bool(case & 1), bool(case & 2)]

            @pl.when(jnp.logical_and(filled[0] == wanted[0], filled[1] == wanted[1]))
            def _(wanted=wanted):
                for c in range(2):
                    ids = ids_ref[2 * chip + c]
                    weights = ids.astype(BF)
                    x = x_ref[2 * chip + c]
                    put(2 * j + c, 0, tile_sum(ids, weights, x, (half * tile).astype(F32), tile))
                    if wanted[c]:
                        value = tile_sum(ids, weights, x, later[c].astype(F32), tile)
                    else:
                        value = jnp.zeros((tile, columns), F32)
                    put(2 * j + c, tile, value)

        return carry

    lax.fori_loop(0, 4, chip_sums, 0)


def sums_body(jobs, afters, old, bound_hbm, ids_ref, x_ref, *refs):
    refs = list(refs)
    take = lambda n: [refs.pop(0) for _ in range(n)]
    inputs = [(take(adds), take(extras)) for _, _, adds, extras in jobs]
    old_in = take(3 if old else 0)
    take(afters)
    outs = take(len(jobs))
    old_out = take(3 if old else 0)
    bound_ref, sem = take(2)
    bound_copy = pltpu.make_async_copy(bound_hbm, bound_ref, sem)
    bound_copy.start()
    if old:
        row_hbm, emb_hbm, acc_hbm = old_in
        old_ref, old_acc_ref, table_ref = old_out
        row_ref, acc_ref, sems = take(3)
        loads = [
            pltpu.make_async_copy(row_hbm, row_ref, sems.at[0]),
            pltpu.make_async_copy(acc_hbm, acc_ref, sems.at[1]),
            pltpu.make_async_copy(emb_hbm, table_ref, sems.at[2]),
        ]
        for load in loads:
            load.start()
    bound_copy.wait()
    for (own, step, _, _), (add, extra), out in zip(jobs, inputs, outs):
        half_sums(own, step, add[0] if add else None, extra[0] if extra else None, out, bound_ref, ids_ref, x_ref)
    if old:
        for load in loads:
            load.wait()

        def gather(i, carry):
            for j in range(8):
                u = i * 8 + j
                row = row_ref[0, u]
                old_ref[pl.ds(u, 1), :] = table_ref[pl.ds(row, 1), :]
                old_acc_ref[0, u] = acc_ref[0, row]
            return carry

        lax.fori_loop(0, old_ref.shape[0] // 8, gather, 0)


def sums(name, bound, ids, xt, slots, jobs, after=(), old=()):
    columns = xt.shape[2]
    shapes, operands, kinds = [], [], []
    for own, step, add, extra, kind in jobs:
        operands += [a for a in (add, extra) if a is not None]
        kinds.append((own, step, int(add is not None), int(extra is not None)))
        shapes.append(jax.ShapeDtypeStruct((8, slots, columns), kind))
    out_specs = [VMEM] * len(shapes)
    scratch = [pltpu.SMEM(bound.shape, jnp.int32), pltpu.SemaphoreType.DMA]
    if old:
        rows, embedding, accumulator = old
        shapes += [
            jax.ShapeDtypeStruct((rows.shape[1], columns), F32),
            jax.ShapeDtypeStruct(rows.shape, F32),
            jax.ShapeDtypeStruct(embedding.shape, F32),
        ]
        out_specs += [VMEM, SMEM, VMEM]
        scratch += [
            pltpu.SMEM(rows.shape, jnp.int32),
            pltpu.SMEM(accumulator.shape, F32),
            pltpu.SemaphoreType.DMA((3,)),
        ]
    return pl.pallas_call(
        functools.partial(sums_body, tuple(kinds), len(after), bool(old)),
        in_specs=[ANY, VMEM, VMEM] + [VMEM] * len(operands) + [ANY] * (len(old) + len(after)),
        out_specs=out_specs,
        out_shape=shapes,
        scratch_shapes=scratch,
        compiler_params=pltpu.CompilerParams(vmem_limit_bytes=12 * MIB),
        cost_estimate=COST,
        name=name,
    )(bound, ids, xt, *operands, *old, *after)


def fold_body(here_ref, back_ref, next_ref, *out_refs):
    place = ring_pos(lax.axis_index("core"))[1]
    for d, out_ref in enumerate(out_refs):
        j = lax.rem(place + d, 4)
        for c in range(2):
            m = 2 * j + c
            value = here_ref[m] + (back_ref[m].astype(F32) + next_ref[m].astype(F32))
            out_ref[c] = value.astype(out_ref.dtype)


def fold(here, back, following):
    shape = (2,) + here.shape[1:]
    return pl.pallas_call(
        fold_body,
        in_specs=[VMEM] * 3,
        out_specs=[VMEM] * 4,
        out_shape=[jax.ShapeDtypeStruct(shape, k) for k in (F32, BF, BF, BF)],
        compiler_params=pltpu.CompilerParams(vmem_limit_bytes=12 * MIB),
        cost_estimate=COST,
        name="fold",
    )(here, back, following)


def total_body(a_ref, b_ref, c_ref, d_ref, mine_ref, other_ref):
    core = lax.axis_index("core")
    for out_ref, table in ((other_ref, 1 - core), (mine_ref, core)):
        out_ref[...] = (a_ref[table] + b_ref[table].astype(F32)) + (
            c_ref[table].astype(F32) + d_ref[table].astype(F32)
        )


def total(parts):
    return pl.pallas_call(
        total_body,
        in_specs=[VMEM] * 4,
        out_specs=[VMEM] * 2,
        out_shape=[jax.ShapeDtypeStruct(parts[0].shape[1:], F32)] * 2,
        compiler_params=pltpu.CompilerParams(vmem_limit_bytes=8 * MIB),
        cost_estimate=COST,
        name="total",
    )(*parts)


def square_body(mine_ref, got_ref, grad_ref, square_ref):
    core = lax.axis_index("core")
    slots = mine_ref.shape[0]
    tile = slots // 2
    for i, (ref, half) in enumerate(((mine_ref, core), (got_ref, 1 - core))):
        for at, first in ((0, half * tile), (tile, slots + i * tile)):
            here = pl.ds(pl.multiple_of(first, tile), tile)
            value = ref[at : at + tile, :]
            grad_ref[here, :] = value
            square_ref[:, here] = jnp.sum((value * value).T, axis=0, keepdims=True)


def square(mine, got):
    slots, columns = mine.shape
    return pl.pallas_call(
        square_body,
        in_specs=[VMEM] * 2,
        out_specs=[VMEM] * 2,
        out_shape=[
            jax.ShapeDtypeStruct((2 * slots, columns), F32),
            jax.ShapeDtypeStruct((1, 2 * slots), F32),
        ],
        compiler_params=pltpu.CompilerParams(vmem_limit_bytes=8 * MIB),
        cost_estimate=COST,
        name="square",
    )(mine, got)


def apply_body(
    width, row_ref, live_ref, emb_in, grad_ref, old_ref, s0_ref, s1_ref, old_acc_ref, acc_in,
    emb_out, acc_out, emb_ref, new_ref, new_acc_ref, new_acc_smem, acc_smem, sems,
):
    load = pltpu.make_async_copy(acc_in, acc_smem, sems.at[0])
    load.start()
    emb_ref[...] = emb_in[...]
    slots, columns = old_ref.shape
    mean_square = (s0_ref[...] + s1_ref[...]) / width
    new_acc = old_acc_ref[...] + mean_square
    new_acc_ref[...] = new_acc
    move = pltpu.make_async_copy(new_acc_ref, new_acc_smem, sems.at[1])
    move.start()
    scale = learn_rate / (jnp.sqrt(new_acc) + epsilon)
    scale = jnp.broadcast_to(scale, (columns, slots)).T
    new_ref[...] = old_ref[...] - grad_ref[...] * scale
    live = live_ref[0]

    def step(i, carry):
        for j in range(8):
            u = jnp.minimum(i * 8 + j, live - 1)
            emb_ref[pl.ds(row_ref[0, u], 1), :] = new_ref[pl.ds(u, 1), :]
        return carry

    lax.fori_loop(0, (live + 7) // 8, step, 0)
    load.wait()
    move.wait()
    write = pltpu.make_async_copy(emb_ref, emb_out, sems.at[2])
    write.start()

    def acc_step(i, carry):
        for j in range(8):
            u = jnp.minimum(i * 8 + j, live - 1)
            acc_smem[0, row_ref[0, u]] = new_acc_smem[0, u]
        return carry

    lax.fori_loop(0, (live + 7) // 8, acc_step, 0)
    store = pltpu.make_async_copy(acc_smem, acc_out, sems.at[0])
    store.start()
    store.wait()
    write.wait()


def apply_rows(width, rows, live, embedding, gradient, old, squares, old_acc, accumulator):
    slots = rows.shape[1]
    return pl.pallas_call(
        functools.partial(apply_body, width),
        in_specs=[SMEM, SMEM] + [VMEM] * 6 + [ANY],
        out_specs=[ANY, ANY],
        out_shape=[
            jax.ShapeDtypeStruct(embedding.shape, F32),
            jax.ShapeDtypeStruct(accumulator.shape, F32),
        ],
        scratch_shapes=[
            pltpu.VMEM(embedding.shape, F32),
            pltpu.VMEM(old.shape, F32),
            pltpu.VMEM((1, slots), F32),
            pltpu.SMEM((1, slots), F32),
            pltpu.SMEM(accumulator.shape, F32),
            pltpu.SemaphoreType.DMA((3,)),
        ],
        compiler_params=pltpu.CompilerParams(vmem_limit_bytes=16 * MIB),
        cost_estimate=COST,
        name="apply_rows",
    )(rows, live, embedding, gradient, old, *squares, old_acc, accumulator)


def per_device(pooled_grad, segment_map, unique_rows, live_counts, embedding, accumulator):
    columns = pooled_grad.shape[2]
    slots = unique_rows.shape[1]
    cols = lax.axis_size("col")
    half = slots // 2
    seg = jnp.transpose(segment_map, (1, 2, 0))
    xt, ids, bound = prep(pooled_grad, seg)

    chips = [(z, y) for z in range(4) for y in range(4)]
    index = lambda z, y, c: ((z % 4) * 4 + y % 4) * 2 + c
    owner = ("z", "y", "core")

    def swap(a):
        return lax.ppermute(a, "core", [(0, 1), (1, 0)])

    def shift(a, first, by):
        move = lambda z, y, c: (z + by, y, c) if (c == 0) == first else (z, y + by, c)
        return lax.ppermute(a, owner, [(index(z, y, c), index(*move(z, y, c))) for z, y in chips for c in range(2)])

    run = lambda name, *jobs, **kw: sums(name, bound, ids, xt, half, jobs, **kw)
    sib = lambda step: (False, step, None, None, BF)
    own = lambda step, add, extra=None, kind=BF: (True, step, add, extra, kind)
    (sib_far,) = run("sib_far", sib(2))
    got_far = swap(sib_far)
    sib_next, sib_back = run("sib_next", sib(1), sib(3), after=(sib_far,))
    got_next, got_back = swap(sib_next), swap(sib_back)
    (far,) = run("own_far", own(2, got_far), after=(sib_next,))
    far_got = shift(far, True, 1)
    sib_here, back = run("middle", sib(0), own(3, got_back), after=(far,))
    got_here = swap(sib_here)
    back_got = shift(back, True, -1)
    (following,) = run("own_next", own(1, got_next, far_got), after=(back,))
    next_got = shift(following, True, 1)
    here, old, old_acc, table = run(
        "own_here", own(0, got_here, None, F32), after=(following,), old=(unique_rows, embedding[0], accumulator)
    )
    parts = list(fold(here, back_got, next_got))
    for d in range(1, 4):
        parts[d] = shift(parts[d], False, d)
    mine, other = total(parts)
    gradient, squares = square(mine, swap(other))
    across = lambda a, k: lax.ppermute(a, "col", [(i, i ^ k) for i in range(cols)])
    pair = squares + across(squares, 1)
    squares = (pair, across(pair, 3))
    new_embedding, new_accumulator = apply_rows(
        columns * cols, unique_rows, live_counts, table, gradient, old, squares, old_acc, accumulator
    )
    return (new_embedding[None], new_accumulator)


def solution(mesh):
    owner = ("z", "y", "core")
    split = Mesh(mesh.devices.reshape(4, 4, 2, mesh.devices.shape[1]), owner + ("col",))
    return jax.shard_map(
        per_device,
        mesh=split,
        in_specs=(
            P(owner, None, "col"),
            P(owner, None, None),
            P(owner, None),
            P(owner),
            P(owner, None, "col"),
            P(owner, None),
        ),
        out_specs=(P(owner, None, "col"), P(owner, None)),
        check_vma=False,
    )
```

```python
import functools

import jax
import jax.numpy as jnp
from jax import lax
from jax.experimental import pallas as pl
from jax.experimental.pallas import tpu as pltpu
from jax.sharding import Mesh
from jax.sharding import PartitionSpec as P

learn_rate = 0.5
epsilon = 1e-08
MIB = 2**20
SCALE = 2.0
BF = jnp.bfloat16
F32 = jnp.float32
VMEM = pl.BlockSpec(memory_space=pltpu.VMEM)
SMEM = pl.BlockSpec(memory_space=pltpu.SMEM)
ANY = pl.BlockSpec(memory_space=pl.ANY)


def cost(us):
    return pl.CostEstimate(flops=int(us * SCALE * 1.15e9), transcendentals=0, bytes_accessed=int(us * SCALE * 3.6e6))


def prep_body(x_hbm, seg_hbm, o_ref, ids_ref, bound_ref, x_ref, seg_ref, sems):
    batch = x_ref.shape[0]
    block = 128
    blocks = batch // block
    seg_copy = pltpu.make_async_copy(seg_hbm, seg_ref, sems.at[blocks])
    seg_copy.start()
    copies = []
    for i in range(blocks):
        here = pl.ds(i * block, block)
        copies.append(pltpu.make_async_copy(x_hbm.at[here], x_ref.at[here], sems.at[i]))
        copies[-1].start()
    seg_copy.wait()
    for t in range(seg_ref.shape[0]):
        last = jnp.max(seg_ref[t], axis=(0, 1), keepdims=True)
        bound_ref[t : t + 1, :] = jnp.broadcast_to(last, (1, bound_ref.shape[1]))
    seg = [seg_ref[:, h, :] for h in range(4)]
    same = lambda a, b: jnp.where(seg[a] == seg[b], 1, 0)
    e01, e02, e03 = same(0, 1), same(0, 2), same(0, 3)
    e12, e13, e23 = same(1, 2), same(1, 3), same(2, 3)
    rows = [
        seg[0],
        jnp.where(e01 > 0, -1, seg[1]),
        jnp.where(e02 + e12 > 0, -1, seg[2]),
        jnp.where(e03 + e13 + e23 > 0, -1, seg[3]),
        1 + e01 + e02 + e03,
        1 + e12 + e13,
        1 + e23,
        jnp.ones_like(e01),
    ]
    for r, value in enumerate(rows):
        ids_ref[:, r, :] = value.astype(F32)
    for i in range(blocks):
        here = pl.ds(i * block, block)
        copies[i].wait()
        o_ref[:, here, :] = jnp.swapaxes(x_ref[here], 0, 1)


def prep(pooled, seg):
    batch, tables, columns = pooled.shape
    return pl.pallas_call(
        prep_body,
        in_specs=[pl.BlockSpec(memory_space=pltpu.HBM)] * 2,
        out_specs=[VMEM] * 3,
        out_shape=[
            jax.ShapeDtypeStruct((tables, batch, columns), BF),
            jax.ShapeDtypeStruct((tables, 8, batch), F32),
            jax.ShapeDtypeStruct((tables, 128), jnp.int32),
        ],
        scratch_shapes=[
            pltpu.VMEM(pooled.shape, BF),
            pltpu.VMEM(seg.shape, jnp.int32),
            pltpu.SemaphoreType.DMA((batch // 128 + 1,)),
        ],
        compiler_params=pltpu.CompilerParams(vmem_limit_bytes=40 * MIB),
        cost_estimate=cost(4),
        name="prep",
    )(pooled, seg)


def tile_sum(ids, weights, x, first, rows):
    batch = x.shape[0]
    number = lax.broadcasted_iota(jnp.int32, (rows, batch), 0).astype(F32).astype(BF)
    local = (ids - first).astype(BF)
    hit = jnp.zeros((rows, batch), BF)
    for h in range(3, -1, -1):
        here = number == jnp.broadcast_to(local[h : h + 1], (rows, batch))
        hit = jnp.where(here, jnp.broadcast_to(weights[4 + h : 5 + h], (rows, batch)), hit)
    return jnp.dot(hit, x, preferred_element_type=F32)


def ring_pos(half):
    at_z, at_y = lax.axis_index("z"), lax.axis_index("y")
    return jnp.where(half == 0, at_z, at_y), jnp.where(half == 0, at_y, at_z)


def half_sums(own, step, parts, add_ref, extra_ref, out_refs, bound_ref, flag_ref, ids_ref, x_ref):
    core = lax.axis_index("core")
    half = core if own else 1 - core
    place = lax.rem(ring_pos(half)[0] + step, 4)
    columns = out_refs[0].shape[2]
    tile = 256
    slots = 2 * tile

    def put(m, part, value):
        here = pl.ds(part * tile, tile)
        if add_ref is not None:
            value = value + add_ref[m, here, :].astype(F32)
        if extra_ref is not None:
            value = value + extra_ref[m].astype(F32)
        if len(out_refs) == len(parts):
            out_refs[parts.index(part)][m] = value.astype(BF)
        else:
            out_refs[0][m, here, :] = value.astype(out_refs[0].dtype)

    def chip_of(j):
        return jnp.where(half == 0, place * 4 + j, j * 4 + place)

    later = [slots + lax.rem(half + c, 2) * tile for c in range(2)]
    if 1 in parts:
        for j in range(4):
            for c in range(2):
                last = jnp.max(bound_ref[pl.ds(2 * chip_of(j) + c, 1), :])
                flag_ref[2 * j + c] = (last >= later[c]).astype(jnp.int32)

    def chip_sums(j, carry):
        chip = chip_of(j)

        def table_sums(wanted):
            for c in range(2):
                ids = ids_ref[2 * chip + c]
                weights = ids.astype(BF)
                x = x_ref[2 * chip + c]
                if 0 in parts:
                    put(2 * j + c, 0, tile_sum(ids, weights, x, (half * tile).astype(F32), tile))
                if 1 in parts:
                    if wanted[c]:
                        value = tile_sum(ids, weights, x, later[c].astype(F32), tile)
                    else:
                        value = jnp.zeros((tile, columns), F32)
                    put(2 * j + c, 1, value)

        if 1 not in parts:
            table_sums((False, False))
            return carry
        filled = [flag_ref[2 * j + c] == 1 for c in range(2)]
        for case in range(4):
            wanted = (bool(case & 1), bool(case & 2))
            here = jnp.logical_and(filled[0] == wanted[0], filled[1] == wanted[1])
            pl.when(here)(functools.partial(table_sums, wanted))
        return carry

    lax.fori_loop(0, 4, chip_sums, 0)


def sums_body(jobs, afters, bound_ref, ids_ref, x_ref, *refs):
    refs = list(refs)
    take = lambda n: [refs.pop(0) for _ in range(n)]
    inputs = [[take(1)[0] if has else None for has in given] for _, _, _, given, _ in jobs]
    take(afters)
    outs = [take(count) for _, _, _, _, count in jobs]
    (flag_ref,) = take(1)
    for (own, step, parts, _, _), (add, extra), out in zip(jobs, inputs, outs):
        half_sums(own, step, parts, add, extra, out, bound_ref, flag_ref, ids_ref, x_ref)


def sums(name, bound, ids, xt, slots, jobs, after=()):
    columns = xt.shape[2]
    shapes, operands, kinds = [], [], []
    for own, step, parts, given, split, kind in jobs:
        operands += [a for a in given if a is not None]
        count = len(parts) if split else 1
        kinds.append((own, step, parts, tuple(a is not None for a in given), count))
        shapes += [jax.ShapeDtypeStruct((8, slots * len(parts) // (2 * count), columns), kind)] * count
    work = sum(len(job[2]) for job in jobs)
    return pl.pallas_call(
        functools.partial(sums_body, tuple(kinds), len(after)),
        in_specs=[VMEM] * (3 + len(operands)) + [ANY] * len(after),
        out_specs=[VMEM] * len(shapes),
        out_shape=shapes,
        scratch_shapes=[pltpu.SMEM((8,), jnp.int32)],
        compiler_params=pltpu.CompilerParams(vmem_limit_bytes=12 * MIB),
        cost_estimate=cost(2 * work),
        name=name,
    )(bound, ids, xt, *operands, *after)


def old_body(row_hbm, emb_hbm, acc_hbm, after_ref, old_ref, old_acc_ref, table_ref, row_ref, acc_ref, sems):
    loads = [
        pltpu.make_async_copy(row_hbm, row_ref, sems.at[0]),
        pltpu.make_async_copy(acc_hbm, acc_ref, sems.at[1]),
        pltpu.make_async_copy(emb_hbm, table_ref, sems.at[2]),
    ]
    for load in loads:
        load.start()
    for load in loads:
        load.wait()

    def gather(i, carry):
        for j in range(8):
            u = i * 8 + j
            row = row_ref[0, u]
            old_ref[pl.ds(u, 1), :] = table_ref[pl.ds(row, 1), :]
            old_acc_ref[0, u] = acc_ref[0, row]
        return carry

    lax.fori_loop(0, old_ref.shape[0] // 8, gather, 0)


def old_values(rows, embedding, accumulator, after):
    return pl.pallas_call(
        old_body,
        in_specs=[ANY] * 4,
        out_specs=[VMEM, SMEM, VMEM],
        out_shape=[
            jax.ShapeDtypeStruct((rows.shape[1], embedding.shape[1]), F32),
            jax.ShapeDtypeStruct(rows.shape, F32),
            jax.ShapeDtypeStruct(embedding.shape, F32),
        ],
        scratch_shapes=[
            pltpu.SMEM(rows.shape, jnp.int32),
            pltpu.SMEM(accumulator.shape, F32),
            pltpu.SemaphoreType.DMA((3,)),
        ],
        compiler_params=pltpu.CompilerParams(vmem_limit_bytes=12 * MIB),
        cost_estimate=cost(4),
        name="old_values",
    )(rows, embedding, accumulator, after)


def fold_body(here_ref, next_low, next_high, back_low, back_high, *out_refs):
    place = ring_pos(lax.axis_index("core"))[1]
    tile = next_low.shape[1]
    for d, out_ref in enumerate(out_refs):
        j = lax.rem(place + d, 4)
        for c in range(2):
            m = 2 * j + c
            for part, (next_ref, back_ref) in enumerate(((next_low, back_low), (next_high, back_high))):
                here = pl.ds(part * tile, tile)
                value = here_ref[m, here, :] + (next_ref[m].astype(F32) + back_ref[m].astype(F32))
                out_ref[c, here, :] = value.astype(out_ref.dtype)


def fold(here, *pieces):
    shape = (2,) + here.shape[1:]
    return pl.pallas_call(
        fold_body,
        in_specs=[VMEM] * 5,
        out_specs=[VMEM] * 4,
        out_shape=[jax.ShapeDtypeStruct(shape, k) for k in (F32, BF, BF, BF)],
        compiler_params=pltpu.CompilerParams(vmem_limit_bytes=12 * MIB),
        cost_estimate=cost(0.4),
        name="fold",
    )(here, *pieces)


def total_body(a_ref, b_ref, c_ref, d_ref, after_ref, mine_ref, other_ref):
    core = lax.axis_index("core")
    for out_ref, table in ((other_ref, 1 - core), (mine_ref, core)):
        out_ref[...] = (a_ref[table] + b_ref[table].astype(F32)) + (
            c_ref[table].astype(F32) + d_ref[table].astype(F32)
        )


def total(parts, after):
    return pl.pallas_call(
        total_body,
        in_specs=[VMEM] * 4 + [ANY],
        out_specs=[VMEM] * 2,
        out_shape=[jax.ShapeDtypeStruct(parts[0].shape[1:], F32)] * 2,
        compiler_params=pltpu.CompilerParams(vmem_limit_bytes=8 * MIB),
        cost_estimate=cost(0.3),
        name="total",
    )(*parts, after)


def square_body(mine_ref, got_ref, grad_ref, square_ref):
    core = lax.axis_index("core")
    slots = mine_ref.shape[0]
    tile = slots // 2
    for i, (ref, half) in enumerate(((mine_ref, core), (got_ref, 1 - core))):
        for at, first in ((0, half * tile), (tile, slots + i * tile)):
            here = pl.ds(pl.multiple_of(first, tile), tile)
            value = ref[at : at + tile, :]
            grad_ref[here, :] = value
            square_ref[:, here] = jnp.sum((value * value).T, axis=0, keepdims=True)


def square(mine, got):
    slots, columns = mine.shape
    return pl.pallas_call(
        square_body,
        in_specs=[VMEM] * 2,
        out_specs=[VMEM] * 2,
        out_shape=[
            jax.ShapeDtypeStruct((2 * slots, columns), F32),
            jax.ShapeDtypeStruct((1, 2 * slots), F32),
        ],
        compiler_params=pltpu.CompilerParams(vmem_limit_bytes=8 * MIB),
        cost_estimate=cost(0.3),
        name="square",
    )(mine, got)


def apply_body(
    width, row_hbm, live_hbm, emb_in, grad_ref, old_ref, s0_ref, s1_ref, old_acc_ref, acc_in,
    emb_out, acc_out, emb_ref, new_ref, new_acc_ref, new_acc_smem, acc_ref, row_ref, live_ref, sems,
):
    loads = [
        pltpu.make_async_copy(row_hbm, row_ref, sems.at[0]),
        pltpu.make_async_copy(live_hbm, live_ref, sems.at[1]),
        pltpu.make_async_copy(acc_in, acc_ref, sems.at[2]),
    ]
    for load in loads:
        load.start()
    slots, columns = old_ref.shape
    new_acc = old_acc_ref[...] + (s0_ref[...] + s1_ref[...]) / width
    new_acc_ref[...] = new_acc
    loads.append(pltpu.make_async_copy(new_acc_ref, new_acc_smem, sems.at[3]))
    loads[-1].start()
    emb_ref[...] = emb_in[...]
    scale = learn_rate / (jnp.sqrt(new_acc) + epsilon)
    scale = jnp.broadcast_to(scale, (columns, slots)).T
    new_ref[...] = old_ref[...] - grad_ref[...] * scale
    for load in loads:
        load.wait()
    live = live_ref[0]

    def put(u):
        row = row_ref[0, u]
        emb_ref[pl.ds(row, 1), :] = new_ref[pl.ds(u, 1), :]
        acc_ref[0, row] = new_acc_smem[0, u]

    def step(i, carry):
        for j in range(8):
            put(i * 8 + j)
        return carry

    def last(u, carry):
        put(u)
        return carry

    lax.fori_loop(0, live // 8, step, 0)
    lax.fori_loop(live // 8 * 8, live, last, 0)
    stores = [
        pltpu.make_async_copy(emb_ref, emb_out, sems.at[0]),
        pltpu.make_async_copy(acc_ref, acc_out, sems.at[1]),
    ]
    for store in stores:
        store.start()
    for store in stores:
        store.wait()


def apply_rows(width, rows, live, embedding, gradient, old, squares, old_acc, accumulator):
    return pl.pallas_call(
        functools.partial(apply_body, width),
        in_specs=[ANY, ANY] + [VMEM] * 6 + [ANY],
        out_specs=[ANY, ANY],
        out_shape=[
            jax.ShapeDtypeStruct(embedding.shape, F32),
            jax.ShapeDtypeStruct(accumulator.shape, F32),
        ],
        scratch_shapes=[
            pltpu.VMEM(embedding.shape, F32),
            pltpu.VMEM(old.shape, F32),
            pltpu.VMEM(rows.shape, F32),
            pltpu.SMEM(rows.shape, F32),
            pltpu.SMEM(accumulator.shape, F32),
            pltpu.SMEM(rows.shape, jnp.int32),
            pltpu.SMEM(live.shape, jnp.int32),
            pltpu.SemaphoreType.DMA((4,)),
        ],
        compiler_params=pltpu.CompilerParams(vmem_limit_bytes=16 * MIB),
        cost_estimate=cost(6),
        name="apply_rows",
    )(rows, live, embedding, gradient, old, *squares, old_acc, accumulator)


def per_device(pooled_grad, segment_map, unique_rows, live_counts, embedding, accumulator):
    columns = pooled_grad.shape[2]
    slots = unique_rows.shape[1]
    cols = lax.axis_size("col")
    half = slots // 2
    seg = jnp.transpose(segment_map, (1, 2, 0))
    xt, ids, bound = prep(pooled_grad, seg)

    chips = [(z, y) for z in range(4) for y in range(4)]
    index = lambda z, y, c: ((z % 4) * 4 + y % 4) * 2 + c
    owner = ("z", "y", "core")

    def swap(a):
        return lax.ppermute(a, "core", [(0, 1), (1, 0)])

    def shift(a, first, by):
        move = lambda z, y, c: (z + by, y, c) if (c == 0) == first else (z, y + by, c)
        return lax.ppermute(a, owner, [(index(z, y, c), index(*move(z, y, c))) for z, y in chips for c in range(2)])

    run = lambda name, *jobs, **kw: sums(name, bound, ids, xt, half, jobs, **kw)
    both = (0, 1)
    sib = lambda step: (False, step, both, (None, None), False, BF)
    own = lambda step, parts, add, extra=None, split=True, kind=BF: (True, step, parts, (add, extra), split, kind)
    (sib_far,) = run("sib_far", sib(2))
    got_far = swap(sib_far)
    sib_next, sib_back, sib_here = run("sib_next", sib(1), sib(3), sib(0), after=(sib_far,))
    got_next, got_back = swap(sib_next), swap(sib_back)
    far_low, far_high = run("own_far", own(2, both, got_far), after=(sib_next,))
    low_got, high_got = shift(far_low, True, 1), shift(far_high, True, -1)
    next_high, back_low = run("free", own(1, (1,), got_next), own(3, (0,), got_back), after=(far_low,))
    next_high_got, back_low_got = shift(next_high, True, 1), shift(back_low, True, -1)
    next_low, back_high = run(
        "bound", own(1, (0,), got_next, low_got), own(3, (1,), got_back, high_got), after=(next_high,)
    )
    next_low_got, back_high_got = shift(next_low, True, 1), shift(back_high, True, -1)
    got_here = swap(sib_here)
    (here,) = run("own_here", own(0, both, got_here, None, False, F32), after=(next_low,))
    parts = list(fold(here, next_low_got, next_high_got, back_low_got, back_high_got))
    old, old_acc, table = old_values(unique_rows, embedding[0], accumulator, parts[1])
    for d in (3, 1, 2):
        parts[d] = shift(parts[d], False, d)
    mine, other = total(parts, old)
    gradient, squares = square(mine, swap(other))
    across = lambda a, k: lax.ppermute(a, "col", [(i, i ^ k) for i in range(cols)])
    pair = squares + across(squares, 1)
    squares = (pair, across(pair, 3))
    new_embedding, new_accumulator = apply_rows(
        columns * cols, unique_rows, live_counts, table, gradient, old, squares, old_acc, accumulator
    )
    return (new_embedding[None], new_accumulator)


def solution(mesh):
    owner = ("z", "y", "core")
    split = Mesh(mesh.devices.reshape(4, 4, 2, mesh.devices.shape[1]), owner + ("col",))
    return jax.shard_map(
        per_device,
        mesh=split,
        in_specs=(
            P(owner, None, "col"),
            P(owner, None, None),
            P(owner, None),
            P(owner),
            P(owner, None, "col"),
            P(owner, None),
        ),
        out_specs=(P(owner, None, "col"), P(owner, None)),
        check_vma=False,
    )
```

```python
import functools

import jax
import jax.numpy as jnp
from jax import lax
from jax.experimental import pallas as pl
from jax.experimental.pallas import tpu as pltpu
from jax.sharding import Mesh
from jax.sharding import PartitionSpec as P

learn_rate = 0.5
epsilon = 1e-08
MIB = 2**20
GATHER = 20
LAST = 1
SCALE = 2.0
BF = jnp.bfloat16
F32 = jnp.float32
VMEM = pl.BlockSpec(memory_space=pltpu.VMEM)
SMEM = pl.BlockSpec(memory_space=pltpu.SMEM)
ANY = pl.BlockSpec(memory_space=pl.ANY)


def cost(us):
    return pl.CostEstimate(flops=int(us * SCALE * 1.15e9), transcendentals=0, bytes_accessed=int(us * SCALE * 3.6e6))


def prep_body(x_hbm, seg_hbm, o_ref, ids_ref, bound_ref, x_ref, seg_ref, sems):
    batch = x_ref.shape[0]
    block = 128
    blocks = batch // block
    seg_copy = pltpu.make_async_copy(seg_hbm, seg_ref, sems.at[blocks])
    seg_copy.start()
    copies = []
    for i in range(blocks):
        here = pl.ds(i * block, block)
        copies.append(pltpu.make_async_copy(x_hbm.at[here], x_ref.at[here], sems.at[i]))
        copies[-1].start()
    seg_copy.wait()
    for t in range(seg_ref.shape[0]):
        last = jnp.max(seg_ref[t], axis=(0, 1), keepdims=True)
        bound_ref[t : t + 1, :] = jnp.broadcast_to(last, (1, bound_ref.shape[1]))
    seg = [seg_ref[:, h, :] for h in range(4)]
    same = lambda a, b: jnp.where(seg[a] == seg[b], 1, 0)
    e01, e02, e03 = same(0, 1), same(0, 2), same(0, 3)
    e12, e13, e23 = same(1, 2), same(1, 3), same(2, 3)
    rows = [
        seg[0],
        jnp.where(e01 > 0, -1, seg[1]),
        jnp.where(e02 + e12 > 0, -1, seg[2]),
        jnp.where(e03 + e13 + e23 > 0, -1, seg[3]),
        1 + e01 + e02 + e03,
        1 + e12 + e13,
        1 + e23,
        jnp.ones_like(e01),
    ]
    for r, value in enumerate(rows):
        ids_ref[:, r, :] = value.astype(F32)
    for i in range(blocks):
        here = pl.ds(i * block, block)
        copies[i].wait()
        o_ref[:, here, :] = jnp.swapaxes(x_ref[here], 0, 1)


def prep(pooled, seg):
    batch, tables, columns = pooled.shape
    return pl.pallas_call(
        prep_body,
        in_specs=[pl.BlockSpec(memory_space=pltpu.HBM)] * 2,
        out_specs=[VMEM] * 3,
        out_shape=[
            jax.ShapeDtypeStruct((tables, batch, columns), BF),
            jax.ShapeDtypeStruct((tables, 8, batch), F32),
            jax.ShapeDtypeStruct((tables, 128), jnp.int32),
        ],
        scratch_shapes=[
            pltpu.VMEM(pooled.shape, BF),
            pltpu.VMEM(seg.shape, jnp.int32),
            pltpu.SemaphoreType.DMA((batch // 128 + 1,)),
        ],
        compiler_params=pltpu.CompilerParams(vmem_limit_bytes=40 * MIB),
        cost_estimate=cost(4),
        name="prep",
    )(pooled, seg)


def tile_sum(ids, weights, x, first, rows):
    batch = x.shape[0]
    number = lax.broadcasted_iota(jnp.int32, (rows, batch), 0).astype(F32).astype(BF)
    local = (ids - first).astype(BF)
    hit = jnp.zeros((rows, batch), BF)
    for h in range(3, -1, -1):
        here = number == jnp.broadcast_to(local[h : h + 1], (rows, batch))
        hit = jnp.where(here, jnp.broadcast_to(weights[4 + h : 5 + h], (rows, batch)), hit)
    return jnp.dot(hit, x, preferred_element_type=F32)


def ring_pos(half):
    at_z, at_y = lax.axis_index("z"), lax.axis_index("y")
    return jnp.where(half == 0, at_z, at_y), jnp.where(half == 0, at_y, at_z)


def half_sums(own, step, parts, add_ref, extra_ref, out_refs, bound_ref, flag_ref, ids_ref, x_ref):
    core = lax.axis_index("core")
    half = core if own else 1 - core
    place = lax.rem(ring_pos(half)[0] + step, 4)
    columns = out_refs[0].shape[2]
    tile = 256
    slots = 2 * tile

    def put(m, part, value):
        here = pl.ds(part * tile, tile)
        if add_ref is not None:
            value = value + add_ref[m, here, :].astype(F32)
        if extra_ref is not None:
            value = value + extra_ref[m].astype(F32)
        if len(out_refs) == len(parts):
            out_refs[parts.index(part)][m] = value.astype(BF)
        else:
            out_refs[0][m, here, :] = value.astype(out_refs[0].dtype)

    def chip_of(j):
        return jnp.where(half == 0, place * 4 + j, j * 4 + place)

    later = [slots + lax.rem(half + c, 2) * tile for c in range(2)]
    if 1 in parts:
        for j in range(4):
            for c in range(2):
                last = jnp.max(bound_ref[pl.ds(2 * chip_of(j) + c, 1), :])
                flag_ref[2 * j + c] = (last >= later[c]).astype(jnp.int32)

    def chip_sums(j, carry):
        chip = chip_of(j)

        def table_sums(wanted):
            for c in range(2):
                ids = ids_ref[2 * chip + c]
                weights = ids.astype(BF)
                x = x_ref[2 * chip + c]
                if 0 in parts:
                    put(2 * j + c, 0, tile_sum(ids, weights, x, (half * tile).astype(F32), tile))
                if 1 in parts:
                    if wanted[c]:
                        value = tile_sum(ids, weights, x, later[c].astype(F32), tile)
                    else:
                        value = jnp.zeros((tile, columns), F32)
                    put(2 * j + c, 1, value)

        if 1 not in parts:
            table_sums((False, False))
            return carry
        filled = [flag_ref[2 * j + c] == 1 for c in range(2)]
        for case in range(4):
            wanted = (bool(case & 1), bool(case & 2))
            here = jnp.logical_and(filled[0] == wanted[0], filled[1] == wanted[1])
            pl.when(here)(functools.partial(table_sums, wanted))
        return carry

    lax.fori_loop(0, 4, chip_sums, 0)


def sums_body(jobs, afters, bound_ref, ids_ref, x_ref, *refs):
    refs = list(refs)
    take = lambda n: [refs.pop(0) for _ in range(n)]
    inputs = [[take(1)[0] if has else None for has in given] for _, _, _, given, _ in jobs]
    take(afters)
    outs = [take(count) for _, _, _, _, count in jobs]
    (flag_ref,) = take(1)
    for (own, step, parts, _, _), (add, extra), out in zip(jobs, inputs, outs):
        half_sums(own, step, parts, add, extra, out, bound_ref, flag_ref, ids_ref, x_ref)


def sums(name, bound, ids, xt, slots, jobs, after=()):
    columns = xt.shape[2]
    shapes, operands, kinds = [], [], []
    for own, step, parts, given, split, kind in jobs:
        operands += [a for a in given if a is not None]
        count = len(parts) if split else 1
        kinds.append((own, step, parts, tuple(a is not None for a in given), count))
        shapes += [jax.ShapeDtypeStruct((8, slots * len(parts) // (2 * count), columns), kind)] * count
    work = sum(len(job[2]) for job in jobs)
    return pl.pallas_call(
        functools.partial(sums_body, tuple(kinds), len(after)),
        in_specs=[VMEM] * (3 + len(operands)) + [ANY] * len(after),
        out_specs=[VMEM] * len(shapes),
        out_shape=shapes,
        scratch_shapes=[pltpu.SMEM((8,), jnp.int32)],
        compiler_params=pltpu.CompilerParams(vmem_limit_bytes=12 * MIB),
        cost_estimate=cost(2 * work if name != "own_here" else LAST),
        name=name,
    )(bound, ids, xt, *operands, *after)


def old_body(row_hbm, emb_hbm, acc_hbm, after_ref, old_ref, old_acc_ref, table_ref, row_ref, acc_ref, sems):
    loads = [
        pltpu.make_async_copy(row_hbm, row_ref, sems.at[0]),
        pltpu.make_async_copy(acc_hbm, acc_ref, sems.at[1]),
        pltpu.make_async_copy(emb_hbm, table_ref, sems.at[2]),
    ]
    for load in loads:
        load.start()
    for load in loads:
        load.wait()

    def gather(i, carry):
        for j in range(8):
            u = i * 8 + j
            row = row_ref[0, u]
            old_ref[pl.ds(u, 1), :] = table_ref[pl.ds(row, 1), :]
            old_acc_ref[0, u] = acc_ref[0, row]
        return carry

    lax.fori_loop(0, old_ref.shape[0] // 8, gather, 0)


def old_values(rows, embedding, accumulator, after):
    return pl.pallas_call(
        old_body,
        in_specs=[ANY] * 4,
        out_specs=[VMEM, SMEM, VMEM],
        out_shape=[
            jax.ShapeDtypeStruct((rows.shape[1], embedding.shape[1]), F32),
            jax.ShapeDtypeStruct(rows.shape, F32),
            pltpu.VMEM(embedding.shape, F32),
        ],
        scratch_shapes=[
            pltpu.SMEM(rows.shape, jnp.int32),
            pltpu.SMEM(accumulator.shape, F32),
            pltpu.SemaphoreType.DMA((3,)),
        ],
        compiler_params=pltpu.CompilerParams(vmem_limit_bytes=12 * MIB),
        cost_estimate=cost(4),
        name="old_values",
    )(rows, embedding, accumulator, after)


def gather_body(here_ref, next_low, next_high, back_low, back_high, out_ref):
    tile = next_low.shape[1]
    for part, (next_ref, back_ref) in enumerate(((next_low, back_low), (next_high, back_high))):
        here = pl.ds(part * tile, tile)
        out_ref[:, here, :] = here_ref[:, here, :] + (next_ref[...].astype(F32) + back_ref[...].astype(F32))


def gather(here, *pieces):
    return pl.pallas_call(
        gather_body,
        in_specs=[VMEM] * 5,
        out_specs=VMEM,
        out_shape=jax.ShapeDtypeStruct(here.shape, F32),
        compiler_params=pltpu.CompilerParams(vmem_limit_bytes=12 * MIB),
        cost_estimate=cost(GATHER),
        name="gather",
    )(here, *pieces)


def fold_body(here_ref, got_ref, *out_refs):
    place = ring_pos(lax.axis_index("core"))[1]
    for d, out_ref in enumerate(out_refs):
        j = lax.rem(place + d, 4)
        for c in range(2):
            m = 2 * j + c
            out_ref[c] = (here_ref[m] + got_ref[m].astype(F32)).astype(out_ref.dtype)


def fold(here, got):
    shape = (2,) + here.shape[1:]
    return pl.pallas_call(
        fold_body,
        in_specs=[VMEM] * 2,
        out_specs=[VMEM] * 4,
        out_shape=[jax.ShapeDtypeStruct(shape, k) for k in (F32, BF, BF, BF)],
        compiler_params=pltpu.CompilerParams(vmem_limit_bytes=12 * MIB),
        cost_estimate=cost(0.4),
        name="fold",
    )(here, got)


def total_body(a_ref, b_ref, c_ref, d_ref, after_ref, mine_ref, other_ref):
    core = lax.axis_index("core")
    for out_ref, table in ((other_ref, 1 - core), (mine_ref, core)):
        out_ref[...] = (a_ref[table] + b_ref[table].astype(F32)) + (
            c_ref[table].astype(F32) + d_ref[table].astype(F32)
        )


def total(parts, after):
    return pl.pallas_call(
        total_body,
        in_specs=[VMEM] * 4 + [ANY],
        out_specs=[VMEM] * 2,
        out_shape=[jax.ShapeDtypeStruct(parts[0].shape[1:], F32)] * 2,
        compiler_params=pltpu.CompilerParams(vmem_limit_bytes=8 * MIB),
        cost_estimate=cost(0.3),
        name="total",
    )(*parts, after)


def square_body(mine_ref, got_ref, grad_ref, square_ref):
    core = lax.axis_index("core")
    slots = mine_ref.shape[0]
    tile = slots // 2
    for i, (ref, half) in enumerate(((mine_ref, core), (got_ref, 1 - core))):
        for at, first in ((0, half * tile), (tile, slots + i * tile)):
            here = pl.ds(pl.multiple_of(first, tile), tile)
            value = ref[at : at + tile, :]
            grad_ref[here, :] = value
            square_ref[:, here] = jnp.sum((value * value).T, axis=0, keepdims=True)


def square(mine, got):
    slots, columns = mine.shape
    return pl.pallas_call(
        square_body,
        in_specs=[VMEM] * 2,
        out_specs=[VMEM] * 2,
        out_shape=[
            jax.ShapeDtypeStruct((2 * slots, columns), F32),
            jax.ShapeDtypeStruct((1, 2 * slots), F32),
        ],
        compiler_params=pltpu.CompilerParams(vmem_limit_bytes=8 * MIB),
        cost_estimate=cost(0.3),
        name="square",
    )(mine, got)


def apply_body(
    width, row_hbm, live_hbm, emb_in, grad_ref, old_ref, s0_ref, s1_ref, old_acc_ref, acc_in,
    emb_out, acc_out, emb_ref, new_ref, new_acc_ref, new_acc_smem, acc_ref, row_ref, live_ref, sems,
):
    loads = [
        pltpu.make_async_copy(row_hbm, row_ref, sems.at[0]),
        pltpu.make_async_copy(live_hbm, live_ref, sems.at[1]),
        pltpu.make_async_copy(acc_in, acc_ref, sems.at[2]),
    ]
    for load in loads:
        load.start()
    slots, columns = old_ref.shape
    new_acc = old_acc_ref[...] + (s0_ref[...] + s1_ref[...]) / width
    new_acc_ref[...] = new_acc
    loads.append(pltpu.make_async_copy(new_acc_ref, new_acc_smem, sems.at[3]))
    loads[-1].start()
    scale = learn_rate / (jnp.sqrt(new_acc) + epsilon)
    scale = jnp.broadcast_to(scale, (columns, slots)).T
    new_ref[...] = old_ref[...] - grad_ref[...] * scale
    row_load, live_load, acc_load, new_load = loads
    row_load.wait()
    live_load.wait()
    live = live_ref[0]
    block = 16

    def scatter(put):
        def step(i, carry):
            for j in range(block):
                put(i * block + j)
            return carry

        def last(u, carry):
            put(u)
            return carry

        lax.fori_loop(0, live // block, step, 0)
        lax.fori_loop(live // block * block, live, last, 0)

    def put_row(u):
        emb_ref[pl.ds(row_ref[0, u], 1), :] = new_ref[pl.ds(u, 1), :]

    def put_acc(u):
        acc_ref[0, row_ref[0, u]] = new_acc_smem[0, u]

    scatter(put_row)
    emb_store = pltpu.make_async_copy(emb_ref, emb_out, sems.at[0])
    emb_store.start()
    acc_load.wait()
    new_load.wait()
    scatter(put_acc)
    acc_store = pltpu.make_async_copy(acc_ref, acc_out, sems.at[1])
    acc_store.start()
    acc_store.wait()
    emb_store.wait()


def apply_rows(width, rows, live, embedding, gradient, old, squares, old_acc, accumulator):
    return pl.pallas_call(
        functools.partial(apply_body, width),
        in_specs=[ANY, ANY] + [VMEM] * 6 + [ANY],
        out_specs=[ANY, ANY, VMEM],
        out_shape=[
            jax.ShapeDtypeStruct(embedding.shape, F32),
            jax.ShapeDtypeStruct(accumulator.shape, F32),
            pltpu.VMEM(embedding.shape, F32),
        ],
        input_output_aliases={2: 2},
        scratch_shapes=[
            pltpu.VMEM(old.shape, F32),
            pltpu.VMEM(rows.shape, F32),
            pltpu.SMEM(rows.shape, F32),
            pltpu.SMEM(accumulator.shape, F32),
            pltpu.SMEM(rows.shape, jnp.int32),
            pltpu.SMEM(live.shape, jnp.int32),
            pltpu.SemaphoreType.DMA((4,)),
        ],
        compiler_params=pltpu.CompilerParams(vmem_limit_bytes=16 * MIB),
        cost_estimate=cost(6),
        name="apply_rows",
    )(rows, live, pltpu.with_memory_space_constraint(embedding, pltpu.VMEM), gradient, old, *squares, old_acc, accumulator)


def per_device(pooled_grad, segment_map, unique_rows, live_counts, embedding, accumulator):
    columns = pooled_grad.shape[2]
    slots = unique_rows.shape[1]
    cols = lax.axis_size("col")
    half = slots // 2
    seg = jnp.transpose(segment_map, (1, 2, 0))
    seg = pltpu.with_memory_space_constraint(seg, pltpu.HBM)
    xt, ids, bound = prep(pooled_grad, seg)

    chips = [(z, y) for z in range(4) for y in range(4)]
    index = lambda z, y, c: ((z % 4) * 4 + y % 4) * 2 + c
    owner = ("z", "y", "core")

    def swap(a):
        return lax.ppermute(a, "core", [(0, 1), (1, 0)])

    def shift(a, first, by):
        move = lambda z, y, c: (z + by, y, c) if (c == 0) == first else (z, y + by, c)
        return lax.ppermute(a, owner, [(index(z, y, c), index(*move(z, y, c))) for z, y in chips for c in range(2)])

    run = lambda name, *jobs, **kw: sums(name, bound, ids, xt, half, jobs, **kw)
    both = (0, 1)
    sib = lambda step: (False, step, both, (None, None), False, BF)
    own = lambda step, parts, add, extra=None, split=True, kind=BF: (True, step, parts, (add, extra), split, kind)
    (sib_far,) = run("sib_far", sib(2))
    got_far = swap(sib_far)
    sib_next, sib_back = run("sib_next", sib(1), sib(3), after=(sib_far,))
    got_next, got_back = swap(sib_next), swap(sib_back)
    far_low, far_high = run("own_far", own(2, both, got_far), after=(sib_next,))
    low_got, high_got = shift(far_low, True, 1), shift(far_high, True, -1)
    next_high, back_low = run("free", own(1, (1,), got_next), own(3, (0,), got_back), after=(far_low,))
    next_high_got, back_low_got = shift(next_high, True, 1), shift(back_low, True, -1)
    next_low, back_high = run(
        "bound", own(1, (0,), got_next, low_got), own(3, (1,), got_back, high_got), after=(next_high,)
    )
    next_low_got, back_high_got = shift(next_low, True, 1), shift(back_high, True, -1)
    (sib_here,) = run("sib_here", sib(0), after=(next_low,))
    got_here = swap(sib_here)
    (here,) = run("own_here", own(0, both, None, None, False, F32), after=(sib_here,))
    gathered = gather(here, next_low_got, next_high_got, back_low_got, back_high_got)
    parts = list(fold(gathered, got_here))
    old, old_acc, table = old_values(unique_rows, embedding[0], accumulator, parts[1])
    for d in (3, 1, 2):
        parts[d] = shift(parts[d], False, d)
    mine, other = total(parts, old)
    gradient, squares = square(mine, swap(other))
    across = lambda a, k: lax.ppermute(a, "col", [(i, i ^ k) for i in range(cols)])
    pair = squares + across(squares, 1)
    squares = (pair, across(pair, 3))
    new_embedding, new_accumulator, _ = apply_rows(
        columns * cols, unique_rows, live_counts, table, gradient, old, squares, old_acc, accumulator
    )
    return (new_embedding[None], new_accumulator)


def solution(mesh):
    owner = ("z", "y", "core")
    split = Mesh(mesh.devices.reshape(4, 4, 2, mesh.devices.shape[1]), owner + ("col",))
    return jax.shard_map(
        per_device,
        mesh=split,
        in_specs=(
            P(owner, None, "col"),
            P(owner, None, None),
            P(owner, None),
            P(owner),
            P(owner, None, "col"),
            P(owner, None),
        ),
        out_specs=(P(owner, None, "col"), P(owner, None)),
        check_vma=False,
    )
```

```python
import functools

import jax
import jax.numpy as jnp
from jax import lax
from jax.experimental import pallas as pl
from jax.experimental.pallas import tpu as pltpu
from jax.sharding import Mesh
from jax.sharding import PartitionSpec as P

learn_rate = 0.5
epsilon = 1e-08
MIB = 2**20
GATHER = 20
LAST = 1
SCALE = 2.0
BF = jnp.bfloat16
F32 = jnp.float32
VMEM = pl.BlockSpec(memory_space=pltpu.VMEM)
SMEM = pl.BlockSpec(memory_space=pltpu.SMEM)
ANY = pl.BlockSpec(memory_space=pl.ANY)


def cost(us):
    return pl.CostEstimate(flops=int(us * SCALE * 1.15e9), transcendentals=0, bytes_accessed=int(us * SCALE * 3.6e6))


def prep_body(x_hbm, seg_hbm, o_ref, ids_ref, bound_ref, x_ref, seg_ref, sems):
    batch = x_ref.shape[0]
    block = 128
    blocks = batch // block
    seg_copy = pltpu.make_async_copy(seg_hbm, seg_ref, sems.at[blocks])
    seg_copy.start()
    copies = []
    for i in range(blocks):
        here = pl.ds(i * block, block)
        copies.append(pltpu.make_async_copy(x_hbm.at[here], x_ref.at[here], sems.at[i]))
        copies[-1].start()
    seg_copy.wait()
    seg = [seg_ref[:, h, :] for h in range(4)]
    last = jnp.maximum(jnp.maximum(seg[0], seg[1]), jnp.maximum(seg[2], seg[3]))
    bound_ref[...] = jnp.broadcast_to(jnp.max(last, axis=1, keepdims=True), bound_ref.shape)
    same = lambda a, b: jnp.where(seg[a] == seg[b], 1, 0)
    e01, e02, e03 = same(0, 1), same(0, 2), same(0, 3)
    e12, e13, e23 = same(1, 2), same(1, 3), same(2, 3)
    rows = [
        seg[0],
        jnp.where(e01 > 0, -1, seg[1]),
        jnp.where(e02 + e12 > 0, -1, seg[2]),
        jnp.where(e03 + e13 + e23 > 0, -1, seg[3]),
        1 + e01 + e02 + e03,
        1 + e12 + e13,
        1 + e23,
        jnp.ones_like(e01),
    ]
    for r, value in enumerate(rows):
        ids_ref[:, r, :] = value.astype(F32)
    for i in range(blocks):
        here = pl.ds(i * block, block)
        copies[i].wait()
        o_ref[:, here, :] = jnp.swapaxes(x_ref[here], 0, 1)


def prep(pooled, seg):
    batch, tables, columns = pooled.shape
    return pl.pallas_call(
        prep_body,
        in_specs=[pl.BlockSpec(memory_space=pltpu.HBM)] * 2,
        out_specs=[VMEM] * 3,
        out_shape=[
            jax.ShapeDtypeStruct((tables, batch, columns), BF),
            jax.ShapeDtypeStruct((tables, 8, batch), F32),
            jax.ShapeDtypeStruct((tables, 128), jnp.int32),
        ],
        scratch_shapes=[
            pltpu.VMEM(pooled.shape, BF),
            pltpu.VMEM(seg.shape, jnp.int32),
            pltpu.SemaphoreType.DMA((batch // 128 + 1,)),
        ],
        compiler_params=pltpu.CompilerParams(vmem_limit_bytes=40 * MIB),
        cost_estimate=cost(4),
        name="prep",
    )(pooled, seg)


def tile_sum(ids, weights, x, first, rows):
    batch = x.shape[0]
    number = lax.broadcasted_iota(jnp.int32, (rows, batch), 0).astype(F32).astype(BF)
    local = (ids - first).astype(BF)
    hit = jnp.zeros((rows, batch), BF)
    for h in range(3, -1, -1):
        here = number == jnp.broadcast_to(local[h : h + 1], (rows, batch))
        hit = jnp.where(here, jnp.broadcast_to(weights[4 + h : 5 + h], (rows, batch)), hit)
    return jnp.dot(hit, x, preferred_element_type=F32)


def ring_pos(half):
    at_z, at_y = lax.axis_index("z"), lax.axis_index("y")
    return jnp.where(half == 0, at_z, at_y), jnp.where(half == 0, at_y, at_z)


def half_sums(own, step, parts, add_ref, extra_ref, out_refs, bound_ref, flag_ref, ids_ref, x_ref):
    core = lax.axis_index("core")
    half = core if own else 1 - core
    place = lax.rem(ring_pos(half)[0] + step, 4)
    columns = out_refs[0].shape[2]
    tile = 256
    slots = 2 * tile

    def put(m, part, value):
        here = pl.ds(part * tile, tile)
        if add_ref is not None:
            value = value + add_ref[m, here, :].astype(F32)
        if extra_ref is not None:
            value = value + extra_ref[m].astype(F32)
        if len(out_refs) == len(parts):
            out_refs[parts.index(part)][m] = value.astype(BF)
        else:
            out_refs[0][m, here, :] = value.astype(out_refs[0].dtype)

    def chip_of(j):
        return jnp.where(half == 0, place * 4 + j, j * 4 + place)

    later = [slots + lax.rem(half + c, 2) * tile for c in range(2)]
    if 1 in parts:
        for j in range(4):
            for c in range(2):
                last = jnp.max(bound_ref[pl.ds(2 * chip_of(j) + c, 1), :])
                flag_ref[2 * j + c] = (last >= later[c]).astype(jnp.int32)

    def chip_sums(j, carry):
        chip = chip_of(j)

        def table_sums(wanted):
            for c in range(2):
                ids = ids_ref[2 * chip + c]
                weights = ids.astype(BF)
                x = x_ref[2 * chip + c]
                if 0 in parts:
                    put(2 * j + c, 0, tile_sum(ids, weights, x, (half * tile).astype(F32), tile))
                if 1 in parts:
                    if wanted[c]:
                        value = tile_sum(ids, weights, x, later[c].astype(F32), tile)
                    else:
                        value = jnp.zeros((tile, columns), F32)
                    put(2 * j + c, 1, value)

        if 1 not in parts:
            table_sums((False, False))
            return carry
        filled = [flag_ref[2 * j + c] == 1 for c in range(2)]
        for case in range(4):
            wanted = (bool(case & 1), bool(case & 2))
            here = jnp.logical_and(filled[0] == wanted[0], filled[1] == wanted[1])
            pl.when(here)(functools.partial(table_sums, wanted))
        return carry

    lax.fori_loop(0, 4, chip_sums, 0)


def sums_body(jobs, afters, bound_ref, ids_ref, x_ref, *refs):
    refs = list(refs)
    take = lambda n: [refs.pop(0) for _ in range(n)]
    inputs = [[take(1)[0] if has else None for has in given] for _, _, _, given, _ in jobs]
    take(afters)
    outs = [take(count) for _, _, _, _, count in jobs]
    (flag_ref,) = take(1)
    for (own, step, parts, _, _), (add, extra), out in zip(jobs, inputs, outs):
        half_sums(own, step, parts, add, extra, out, bound_ref, flag_ref, ids_ref, x_ref)


def sums(name, bound, ids, xt, slots, jobs, after=()):
    columns = xt.shape[2]
    shapes, operands, kinds = [], [], []
    for own, step, parts, given, split, kind in jobs:
        operands += [a for a in given if a is not None]
        count = len(parts) if split else 1
        kinds.append((own, step, parts, tuple(a is not None for a in given), count))
        shapes += [jax.ShapeDtypeStruct((8, slots * len(parts) // (2 * count), columns), kind)] * count
    work = sum(len(job[2]) for job in jobs)
    return pl.pallas_call(
        functools.partial(sums_body, tuple(kinds), len(after)),
        in_specs=[VMEM] * (3 + len(operands)) + [ANY] * len(after),
        out_specs=[VMEM] * len(shapes),
        out_shape=shapes,
        scratch_shapes=[pltpu.SMEM((8,), jnp.int32)],
        compiler_params=pltpu.CompilerParams(vmem_limit_bytes=12 * MIB),
        cost_estimate=cost(2 * work if name != "own_here" else LAST),
        name=name,
    )(bound, ids, xt, *operands, *after)


def old_body(row_hbm, emb_hbm, acc_hbm, after_ref, old_ref, old_acc_ref, table_ref, row_ref, acc_ref, sems):
    loads = [
        pltpu.make_async_copy(row_hbm, row_ref, sems.at[0]),
        pltpu.make_async_copy(acc_hbm, acc_ref, sems.at[1]),
        pltpu.make_async_copy(emb_hbm, table_ref, sems.at[2]),
    ]
    for load in loads:
        load.start()
    for load in loads:
        load.wait()

    def gather(i, carry):
        for j in range(8):
            u = i * 8 + j
            row = row_ref[0, u]
            old_ref[pl.ds(u, 1), :] = table_ref[pl.ds(row, 1), :]
            old_acc_ref[0, u] = acc_ref[0, row]
        return carry

    lax.fori_loop(0, old_ref.shape[0] // 8, gather, 0)


def old_values(rows, embedding, accumulator, after):
    return pl.pallas_call(
        old_body,
        in_specs=[ANY] * 4,
        out_specs=[VMEM, SMEM, VMEM],
        out_shape=[
            jax.ShapeDtypeStruct((rows.shape[1], embedding.shape[1]), F32),
            jax.ShapeDtypeStruct(rows.shape, F32),
            pltpu.VMEM(embedding.shape, F32),
        ],
        scratch_shapes=[
            pltpu.SMEM(rows.shape, jnp.int32),
            pltpu.SMEM(accumulator.shape, F32),
            pltpu.SemaphoreType.DMA((3,)),
        ],
        compiler_params=pltpu.CompilerParams(vmem_limit_bytes=12 * MIB),
        cost_estimate=cost(4),
        name="old_values",
    )(rows, embedding, accumulator, after)


def gather_body(here_ref, next_low, next_high, back_low, back_high, out_ref):
    tile = next_low.shape[1]
    for part, (next_ref, back_ref) in enumerate(((next_low, back_low), (next_high, back_high))):
        here = pl.ds(part * tile, tile)
        out_ref[:, here, :] = here_ref[:, here, :] + (next_ref[...].astype(F32) + back_ref[...].astype(F32))


def gather(here, *pieces):
    return pl.pallas_call(
        gather_body,
        in_specs=[VMEM] * 5,
        out_specs=VMEM,
        out_shape=jax.ShapeDtypeStruct(here.shape, F32),
        compiler_params=pltpu.CompilerParams(vmem_limit_bytes=12 * MIB),
        cost_estimate=cost(GATHER),
        name="gather",
    )(here, *pieces)


def fold_body(here_ref, got_ref, *out_refs):
    place = ring_pos(lax.axis_index("core"))[1]
    for d, out_ref in enumerate(out_refs):
        j = lax.rem(place + d, 4)
        for c in range(2):
            m = 2 * j + c
            out_ref[c] = (here_ref[m] + got_ref[m].astype(F32)).astype(out_ref.dtype)


def fold(here, got):
    shape = (2,) + here.shape[1:]
    return pl.pallas_call(
        fold_body,
        in_specs=[VMEM] * 2,
        out_specs=[VMEM] * 4,
        out_shape=[jax.ShapeDtypeStruct(shape, k) for k in (F32, BF, BF, BF)],
        compiler_params=pltpu.CompilerParams(vmem_limit_bytes=12 * MIB),
        cost_estimate=cost(0.4),
        name="fold",
    )(here, got)


def total_body(a_ref, b_ref, c_ref, d_ref, after_ref, mine_ref, other_ref):
    core = lax.axis_index("core")
    for out_ref, table in ((other_ref, 1 - core), (mine_ref, core)):
        out_ref[...] = (a_ref[table] + b_ref[table].astype(F32)) + (
            c_ref[table].astype(F32) + d_ref[table].astype(F32)
        )


def total(parts, after):
    return pl.pallas_call(
        total_body,
        in_specs=[VMEM] * 4 + [ANY],
        out_specs=[VMEM] * 2,
        out_shape=[jax.ShapeDtypeStruct(parts[0].shape[1:], F32)] * 2,
        compiler_params=pltpu.CompilerParams(vmem_limit_bytes=8 * MIB),
        cost_estimate=cost(0.3),
        name="total",
    )(*parts, after)


def square_body(mine_ref, got_ref, grad_ref, square_ref):
    core = lax.axis_index("core")
    slots = mine_ref.shape[0]
    tile = slots // 2
    for i, (ref, half) in enumerate(((mine_ref, core), (got_ref, 1 - core))):
        for at, first in ((0, half * tile), (tile, slots + i * tile)):
            here = pl.ds(pl.multiple_of(first, tile), tile)
            value = ref[at : at + tile, :]
            grad_ref[here, :] = value
            square_ref[:, here] = jnp.sum((value * value).T, axis=0, keepdims=True)


def square(mine, got):
    slots, columns = mine.shape
    return pl.pallas_call(
        square_body,
        in_specs=[VMEM] * 2,
        out_specs=[VMEM] * 2,
        out_shape=[
            jax.ShapeDtypeStruct((2 * slots, columns), F32),
            jax.ShapeDtypeStruct((1, 2 * slots), F32),
        ],
        compiler_params=pltpu.CompilerParams(vmem_limit_bytes=8 * MIB),
        cost_estimate=cost(0.3),
        name="square",
    )(mine, got)


def apply_body(
    width, row_hbm, live_hbm, emb_in, grad_ref, old_ref, s0_ref, s1_ref, old_acc_ref, acc_in,
    emb_out, acc_out, emb_ref, new_ref, new_acc_ref, new_acc_smem, acc_ref, row_ref, live_ref, sems,
):
    loads = [
        pltpu.make_async_copy(row_hbm, row_ref, sems.at[0]),
        pltpu.make_async_copy(live_hbm, live_ref, sems.at[1]),
        pltpu.make_async_copy(acc_in, acc_ref, sems.at[2]),
    ]
    for load in loads:
        load.start()
    slots, columns = old_ref.shape
    new_acc = old_acc_ref[...] + (s0_ref[...] + s1_ref[...]) / width
    new_acc_ref[...] = new_acc
    loads.append(pltpu.make_async_copy(new_acc_ref, new_acc_smem, sems.at[3]))
    loads[-1].start()
    scale = learn_rate / (jnp.sqrt(new_acc) + epsilon)
    scale = jnp.broadcast_to(scale, (columns, slots)).T
    new_ref[...] = old_ref[...] - grad_ref[...] * scale
    row_load, live_load, acc_load, new_load = loads
    row_load.wait()
    live_load.wait()
    live = live_ref[0]
    block = 16

    def scatter(put):
        def step(i, carry):
            for j in range(block):
                put(i * block + j)
            return carry

        def last(u, carry):
            put(u)
            return carry

        lax.fori_loop(0, live // block, step, 0)
        lax.fori_loop(live // block * block, live, last, 0)

    def put_row(u):
        emb_ref[pl.ds(row_ref[0, u], 1), :] = new_ref[pl.ds(u, 1), :]

    def put_acc(u):
        acc_ref[0, row_ref[0, u]] = new_acc_smem[0, u]

    scatter(put_row)
    emb_store = pltpu.make_async_copy(emb_ref, emb_out, sems.at[0])
    emb_store.start()
    acc_load.wait()
    new_load.wait()
    scatter(put_acc)
    acc_store = pltpu.make_async_copy(acc_ref, acc_out, sems.at[1])
    acc_store.start()
    acc_store.wait()
    emb_store.wait()


def apply_rows(width, rows, live, embedding, gradient, old, squares, old_acc, accumulator):
    return pl.pallas_call(
        functools.partial(apply_body, width),
        in_specs=[ANY, ANY] + [VMEM] * 6 + [ANY],
        out_specs=[ANY, ANY, VMEM],
        out_shape=[
            jax.ShapeDtypeStruct(embedding.shape, F32),
            jax.ShapeDtypeStruct(accumulator.shape, F32),
            pltpu.VMEM(embedding.shape, F32),
        ],
        input_output_aliases={2: 2},
        scratch_shapes=[
            pltpu.VMEM(old.shape, F32),
            pltpu.VMEM(rows.shape, F32),
            pltpu.SMEM(rows.shape, F32),
            pltpu.SMEM(accumulator.shape, F32),
            pltpu.SMEM(rows.shape, jnp.int32),
            pltpu.SMEM(live.shape, jnp.int32),
            pltpu.SemaphoreType.DMA((4,)),
        ],
        compiler_params=pltpu.CompilerParams(vmem_limit_bytes=16 * MIB),
        cost_estimate=cost(6),
        name="apply_rows",
    )(rows, live, pltpu.with_memory_space_constraint(embedding, pltpu.VMEM), gradient, old, *squares, old_acc, accumulator)


def per_device(pooled_grad, segment_map, unique_rows, live_counts, embedding, accumulator):
    columns = pooled_grad.shape[2]
    slots = unique_rows.shape[1]
    cols = lax.axis_size("col")
    half = slots // 2
    seg = jnp.transpose(segment_map, (1, 2, 0))
    seg = pltpu.with_memory_space_constraint(seg, pltpu.HBM)
    xt, ids, bound = prep(pooled_grad, seg)

    chips = [(z, y) for z in range(4) for y in range(4)]
    index = lambda z, y, c: ((z % 4) * 4 + y % 4) * 2 + c
    owner = ("z", "y", "core")

    def swap(a):
        return lax.ppermute(a, "core", [(0, 1), (1, 0)])

    def shift(a, first, by):
        move = lambda z, y, c: (z + by, y, c) if (c == 0) == first else (z, y + by, c)
        return lax.ppermute(a, owner, [(index(z, y, c), index(*move(z, y, c))) for z, y in chips for c in range(2)])

    run = lambda name, *jobs, **kw: sums(name, bound, ids, xt, half, jobs, **kw)
    both = (0, 1)
    sib = lambda step: (False, step, both, (None, None), False, BF)
    own = lambda step, parts, add, extra=None, split=True, kind=BF: (True, step, parts, (add, extra), split, kind)
    (sib_far,) = run("sib_far", sib(2))
    got_far = swap(sib_far)
    sib_next, sib_back = run("sib_next", sib(1), sib(3), after=(sib_far,))
    got_next, got_back = swap(sib_next), swap(sib_back)
    far_low, far_high = run("own_far", own(2, both, got_far), after=(sib_next,))
    low_got, high_got = shift(far_low, True, 1), shift(far_high, True, -1)
    next_high, back_low = run("free", own(1, (1,), got_next), own(3, (0,), got_back), after=(far_low,))
    next_high_got, back_low_got = shift(next_high, True, 1), shift(back_low, True, -1)
    next_low, back_high = run(
        "bound", own(1, (0,), got_next, low_got), own(3, (1,), got_back, high_got), after=(next_high,)
    )
    next_low_got, back_high_got = shift(next_low, True, 1), shift(back_high, True, -1)
    (sib_here,) = run("sib_here", sib(0), after=(next_low,))
    got_here = swap(sib_here)
    (here,) = run("own_here", own(0, both, None, None, False, F32), after=(sib_here,))
    gathered = gather(here, next_low_got, next_high_got, back_low_got, back_high_got)
    parts = list(fold(gathered, got_here))
    old, old_acc, table = old_values(unique_rows, embedding[0], accumulator, parts[1])
    for d in (3, 1, 2):
        parts[d] = shift(parts[d], False, d)
    mine, other = total(parts, old)
    gradient, squares = square(mine, swap(other))
    across = lambda a, k: lax.ppermute(a, "col", [(i, i ^ k) for i in range(cols)])
    pair = squares + across(squares, 1)
    squares = (pair, across(pair, 3))
    new_embedding, new_accumulator, _ = apply_rows(
        columns * cols, unique_rows, live_counts, table, gradient, old, squares, old_acc, accumulator
    )
    return (new_embedding[None], new_accumulator)


def solution(mesh):
    owner = ("z", "y", "core")
    split = Mesh(mesh.devices.reshape(4, 4, 2, mesh.devices.shape[1]), owner + ("col",))
    return jax.shard_map(
        per_device,
        mesh=split,
        in_specs=(
            P(owner, None, "col"),
            P(owner, None, None),
            P(owner, None),
            P(owner),
            P(owner, None, "col"),
            P(owner, None),
        ),
        out_specs=(P(owner, None, "col"), P(owner, None)),
        check_vma=False,
    )
```

```python
import functools

import jax
import jax.numpy as jnp
from jax import lax
from jax.experimental import pallas as pl
from jax.experimental.pallas import tpu as pltpu
from jax.sharding import Mesh
from jax.sharding import PartitionSpec as P

learn_rate = 0.5
epsilon = 1e-08
MIB = 2**20
GATHER = 20
LAST = 1
SCALE = 2.0
BF = jnp.bfloat16
F32 = jnp.float32
VMEM = pl.BlockSpec(memory_space=pltpu.VMEM)
SMEM = pl.BlockSpec(memory_space=pltpu.SMEM)
ANY = pl.BlockSpec(memory_space=pl.ANY)


def cost(us):
    return pl.CostEstimate(flops=int(us * SCALE * 1.15e9), transcendentals=0, bytes_accessed=int(us * SCALE * 3.6e6))


def prep_body(x_hbm, seg_hbm, o_ref, ids_ref, bound_ref, x_ref, seg_ref, sems):
    batch = x_ref.shape[0]
    block = 128
    blocks = batch // block
    seg_copy = pltpu.make_async_copy(seg_hbm, seg_ref, sems.at[blocks])
    seg_copy.start()
    copies = []
    for i in range(blocks):
        here = pl.ds(i * block, block)
        copies.append(pltpu.make_async_copy(x_hbm.at[here], x_ref.at[here], sems.at[i]))
        copies[-1].start()
    seg_copy.wait()
    seg = [seg_ref[:, h, :] for h in range(4)]
    last = jnp.maximum(jnp.maximum(seg[0], seg[1]), jnp.maximum(seg[2], seg[3]))
    bound_ref[...] = jnp.broadcast_to(jnp.max(last, axis=1, keepdims=True), bound_ref.shape)
    same = lambda a, b: jnp.where(seg[a] == seg[b], 1, 0)
    e01, e02, e03 = same(0, 1), same(0, 2), same(0, 3)
    e12, e13, e23 = same(1, 2), same(1, 3), same(2, 3)
    rows = [
        seg[0],
        jnp.where(e01 > 0, -1, seg[1]),
        jnp.where(e02 + e12 > 0, -1, seg[2]),
        jnp.where(e03 + e13 + e23 > 0, -1, seg[3]),
        1 + e01 + e02 + e03,
        1 + e12 + e13,
        1 + e23,
        jnp.ones_like(e01),
    ]
    for r, value in enumerate(rows):
        ids_ref[:, r, :] = value.astype(F32)
    for i in range(blocks):
        here = pl.ds(i * block, block)
        copies[i].wait()
        o_ref[:, here, :] = jnp.swapaxes(x_ref[here], 0, 1)


def prep(pooled, seg):
    batch, tables, columns = pooled.shape
    return pl.pallas_call(
        prep_body,
        in_specs=[pl.BlockSpec(memory_space=pltpu.HBM)] * 2,
        out_specs=[VMEM] * 3,
        out_shape=[
            jax.ShapeDtypeStruct((tables, batch, columns), BF),
            jax.ShapeDtypeStruct((tables, 8, batch), F32),
            jax.ShapeDtypeStruct((tables, 128), jnp.int32),
        ],
        scratch_shapes=[
            pltpu.VMEM(pooled.shape, BF),
            pltpu.VMEM(seg.shape, jnp.int32),
            pltpu.SemaphoreType.DMA((batch // 128 + 1,)),
        ],
        compiler_params=pltpu.CompilerParams(vmem_limit_bytes=40 * MIB),
        cost_estimate=cost(4),
        name="prep",
    )(pooled, seg)


def tile_sum(ids, weights, x, first, rows):
    batch = x.shape[0]
    number = lax.broadcasted_iota(jnp.int32, (rows, batch), 0).astype(F32).astype(BF)
    local = (ids - first).astype(BF)
    hit = jnp.zeros((rows, batch), BF)
    for h in range(3, -1, -1):
        here = number == jnp.broadcast_to(local[h : h + 1], (rows, batch))
        hit = jnp.where(here, jnp.broadcast_to(weights[4 + h : 5 + h], (rows, batch)), hit)
    return jnp.dot(hit, x, preferred_element_type=F32)


def ring_pos(half):
    at_z, at_y = lax.axis_index("z"), lax.axis_index("y")
    return jnp.where(half == 0, at_z, at_y), jnp.where(half == 0, at_y, at_z)


def half_sums(own, step, parts, add_ref, extra_ref, out_refs, bound_ref, flag_ref, ids_ref, x_ref):
    core = lax.axis_index("core")
    half = core if own else 1 - core
    place = lax.rem(ring_pos(half)[0] + step, 4)
    columns = out_refs[0].shape[2]
    tile = 256
    slots = 2 * tile

    def put(m, part, value):
        here = pl.ds(part * tile, tile)
        if add_ref is not None:
            value = value + add_ref[m, here, :].astype(F32)
        if extra_ref is not None:
            value = value + extra_ref[m].astype(F32)
        if len(out_refs) == len(parts):
            out_refs[parts.index(part)][m] = value.astype(BF)
        else:
            out_refs[0][m, here, :] = value.astype(out_refs[0].dtype)

    def chip_of(j):
        return jnp.where(half == 0, place * 4 + j, j * 4 + place)

    later = [slots + lax.rem(half + c, 2) * tile for c in range(2)]
    if 1 in parts:
        for j in range(4):
            for c in range(2):
                last = jnp.max(bound_ref[pl.ds(2 * chip_of(j) + c, 1), :])
                flag_ref[2 * j + c] = (last >= later[c]).astype(jnp.int32)

    def chip_sums(j, carry):
        chip = chip_of(j)

        def table_sums(wanted):
            for c in range(2):
                ids = ids_ref[2 * chip + c]
                weights = ids.astype(BF)
                x = x_ref[2 * chip + c]
                if 0 in parts:
                    put(2 * j + c, 0, tile_sum(ids, weights, x, (half * tile).astype(F32), tile))
                if 1 in parts:
                    if wanted[c]:
                        value = tile_sum(ids, weights, x, later[c].astype(F32), tile)
                    else:
                        value = jnp.zeros((tile, columns), F32)
                    put(2 * j + c, 1, value)

        if 1 not in parts:
            table_sums((False, False))
            return carry
        filled = [flag_ref[2 * j + c] == 1 for c in range(2)]
        for case in range(4):
            wanted = (bool(case & 1), bool(case & 2))
            here = jnp.logical_and(filled[0] == wanted[0], filled[1] == wanted[1])
            pl.when(here)(functools.partial(table_sums, wanted))
        return carry

    lax.fori_loop(0, 4, chip_sums, 0)


def sums_body(jobs, afters, bound_ref, ids_ref, x_ref, *refs):
    refs = list(refs)
    take = lambda n: [refs.pop(0) for _ in range(n)]
    inputs = [[take(1)[0] if has else None for has in given] for _, _, _, given, _ in jobs]
    take(afters)
    outs = [take(count) for _, _, _, _, count in jobs]
    (flag_ref,) = take(1)
    for (own, step, parts, _, _), (add, extra), out in zip(jobs, inputs, outs):
        half_sums(own, step, parts, add, extra, out, bound_ref, flag_ref, ids_ref, x_ref)


def sums(name, bound, ids, xt, slots, jobs, after=()):
    columns = xt.shape[2]
    shapes, operands, kinds = [], [], []
    for own, step, parts, given, split, kind in jobs:
        operands += [a for a in given if a is not None]
        count = len(parts) if split else 1
        kinds.append((own, step, parts, tuple(a is not None for a in given), count))
        shapes += [jax.ShapeDtypeStruct((8, slots * len(parts) // (2 * count), columns), kind)] * count
    work = sum(len(job[2]) for job in jobs)
    return pl.pallas_call(
        functools.partial(sums_body, tuple(kinds), len(after)),
        in_specs=[VMEM] * (3 + len(operands)) + [ANY] * len(after),
        out_specs=[VMEM] * len(shapes),
        out_shape=shapes,
        scratch_shapes=[pltpu.SMEM((8,), jnp.int32)],
        compiler_params=pltpu.CompilerParams(vmem_limit_bytes=12 * MIB),
        cost_estimate=cost(2 * work if name != "own_here" else LAST),
        name=name,
    )(bound, ids, xt, *operands, *after)


def old_body(row_hbm, emb_hbm, acc_hbm, after_ref, old_ref, old_acc_ref, table_ref, row_ref, acc_ref, sems):
    loads = [
        pltpu.make_async_copy(row_hbm, row_ref, sems.at[0]),
        pltpu.make_async_copy(acc_hbm, acc_ref, sems.at[1]),
        pltpu.make_async_copy(emb_hbm, table_ref, sems.at[2]),
    ]
    for load in loads:
        load.start()
    for load in loads:
        load.wait()

    def gather(i, carry):
        for j in range(8):
            u = i * 8 + j
            row = row_ref[0, u]
            old_ref[pl.ds(u, 1), :] = table_ref[pl.ds(row, 1), :]
            old_acc_ref[0, u] = acc_ref[0, row]
        return carry

    lax.fori_loop(0, old_ref.shape[0] // 8, gather, 0)


def old_values(rows, embedding, accumulator, after):
    return pl.pallas_call(
        old_body,
        in_specs=[ANY] * 4,
        out_specs=[VMEM, SMEM, VMEM],
        out_shape=[
            jax.ShapeDtypeStruct((rows.shape[1], embedding.shape[1]), F32),
            jax.ShapeDtypeStruct(rows.shape, F32),
            pltpu.VMEM(embedding.shape, F32),
        ],
        scratch_shapes=[
            pltpu.SMEM(rows.shape, jnp.int32),
            pltpu.SMEM(accumulator.shape, F32),
            pltpu.SemaphoreType.DMA((3,)),
        ],
        compiler_params=pltpu.CompilerParams(vmem_limit_bytes=12 * MIB),
        cost_estimate=cost(4),
        name="old_values",
    )(rows, embedding, accumulator, after)


def gather_body(here_ref, next_low, next_high, back_low, back_high, out_ref):
    tile = next_low.shape[1]
    for part, (next_ref, back_ref) in enumerate(((next_low, back_low), (next_high, back_high))):
        here = pl.ds(part * tile, tile)
        out_ref[:, here, :] = here_ref[:, here, :] + (next_ref[...].astype(F32) + back_ref[...].astype(F32))


def gather(here, *pieces):
    return pl.pallas_call(
        gather_body,
        in_specs=[VMEM] * 5,
        out_specs=VMEM,
        out_shape=jax.ShapeDtypeStruct(here.shape, F32),
        compiler_params=pltpu.CompilerParams(vmem_limit_bytes=12 * MIB),
        cost_estimate=cost(GATHER),
        name="gather",
    )(here, *pieces)


def fold_body(here_ref, got_ref, *out_refs):
    place = ring_pos(lax.axis_index("core"))[1]
    for d, out_ref in enumerate(out_refs):
        j = lax.rem(place + d, 4)
        for c in range(2):
            m = 2 * j + c
            out_ref[c] = (here_ref[m] + got_ref[m].astype(F32)).astype(out_ref.dtype)


def fold(here, got):
    shape = (2,) + here.shape[1:]
    return pl.pallas_call(
        fold_body,
        in_specs=[VMEM] * 2,
        out_specs=[VMEM] * 4,
        out_shape=[jax.ShapeDtypeStruct(shape, k) for k in (F32, BF, BF, BF)],
        compiler_params=pltpu.CompilerParams(vmem_limit_bytes=12 * MIB),
        cost_estimate=cost(0.4),
        name="fold",
    )(here, got)


def total_body(a_ref, b_ref, c_ref, d_ref, after_ref, mine_ref, other_ref):
    core = lax.axis_index("core")
    for out_ref, table in ((other_ref, 1 - core), (mine_ref, core)):
        out_ref[...] = (a_ref[table] + b_ref[table].astype(F32)) + (
            c_ref[table].astype(F32) + d_ref[table].astype(F32)
        )


def total(parts, after):
    return pl.pallas_call(
        total_body,
        in_specs=[VMEM] * 4 + [ANY],
        out_specs=[VMEM] * 2,
        out_shape=[jax.ShapeDtypeStruct(parts[0].shape[1:], F32)] * 2,
        compiler_params=pltpu.CompilerParams(vmem_limit_bytes=8 * MIB),
        cost_estimate=cost(0.3),
        name="total",
    )(*parts, after)


def square_body(mine_ref, got_ref, grad_ref, square_ref):
    core = lax.axis_index("core")
    slots = mine_ref.shape[0]
    tile = slots // 2
    for i, (ref, half) in enumerate(((mine_ref, core), (got_ref, 1 - core))):
        for at, first in ((0, half * tile), (tile, slots + i * tile)):
            here = pl.ds(pl.multiple_of(first, tile), tile)
            value = ref[at : at + tile, :]
            grad_ref[here, :] = value
            square_ref[:, here] = jnp.sum((value * value).T, axis=0, keepdims=True)


def square(mine, got):
    slots, columns = mine.shape
    return pl.pallas_call(
        square_body,
        in_specs=[VMEM] * 2,
        out_specs=[VMEM] * 2,
        out_shape=[
            jax.ShapeDtypeStruct((2 * slots, columns), F32),
            jax.ShapeDtypeStruct((1, 2 * slots), F32),
        ],
        compiler_params=pltpu.CompilerParams(vmem_limit_bytes=8 * MIB),
        cost_estimate=cost(0.3),
        name="square",
    )(mine, got)


def apply_body(
    width, row_hbm, live_hbm, emb_in, grad_ref, old_ref, s0_ref, s1_ref, old_acc_ref, acc_in,
    emb_out, acc_out, emb_ref, new_ref, new_acc_ref, new_acc_smem, acc_ref, row_ref, live_ref, sems,
):
    loads = [
        pltpu.make_async_copy(row_hbm, row_ref, sems.at[0]),
        pltpu.make_async_copy(live_hbm, live_ref, sems.at[1]),
        pltpu.make_async_copy(acc_in, acc_ref, sems.at[2]),
    ]
    for load in loads:
        load.start()
    slots, columns = old_ref.shape
    new_acc = old_acc_ref[...] + (s0_ref[...] + s1_ref[...]) / width
    new_acc_ref[...] = new_acc
    loads.append(pltpu.make_async_copy(new_acc_ref, new_acc_smem, sems.at[3]))
    loads[-1].start()
    scale = learn_rate / (jnp.sqrt(new_acc) + epsilon)
    scale = jnp.broadcast_to(scale, (columns, slots)).T
    new_ref[...] = old_ref[...] - grad_ref[...] * scale
    row_load, live_load, acc_load, new_load = loads
    row_load.wait()
    live_load.wait()
    live = live_ref[0]
    block = 32

    def scatter(put):
        def step(i, carry):
            for j in range(block):
                put(i * block + j)
            return carry

        def last(u, carry):
            put(u)
            return carry

        lax.fori_loop(0, live // block, step, 0)
        lax.fori_loop(live // block * block, live, last, 0)

    def put_row(u):
        emb_ref[pl.ds(row_ref[0, u], 1), :] = new_ref[pl.ds(u, 1), :]

    def put_acc(u):
        acc_ref[0, row_ref[0, u]] = new_acc_smem[0, u]

    scatter(put_row)
    emb_store = pltpu.make_async_copy(emb_ref, emb_out, sems.at[0])
    emb_store.start()
    acc_load.wait()
    new_load.wait()
    scatter(put_acc)
    acc_store = pltpu.make_async_copy(acc_ref, acc_out, sems.at[1])
    acc_store.start()
    acc_store.wait()
    emb_store.wait()


def apply_rows(width, rows, live, embedding, gradient, old, squares, old_acc, accumulator):
    return pl.pallas_call(
        functools.partial(apply_body, width),
        in_specs=[ANY, ANY] + [VMEM] * 6 + [ANY],
        out_specs=[ANY, ANY, VMEM],
        out_shape=[
            jax.ShapeDtypeStruct(embedding.shape, F32),
            jax.ShapeDtypeStruct(accumulator.shape, F32),
            pltpu.VMEM(embedding.shape, F32),
        ],
        input_output_aliases={2: 2},
        scratch_shapes=[
            pltpu.VMEM(old.shape, F32),
            pltpu.VMEM(rows.shape, F32),
            pltpu.SMEM(rows.shape, F32),
            pltpu.SMEM(accumulator.shape, F32),
            pltpu.SMEM(rows.shape, jnp.int32),
            pltpu.SMEM(live.shape, jnp.int32),
            pltpu.SemaphoreType.DMA((4,)),
        ],
        compiler_params=pltpu.CompilerParams(vmem_limit_bytes=16 * MIB),
        cost_estimate=cost(6),
        name="apply_rows",
    )(rows, live, pltpu.with_memory_space_constraint(embedding, pltpu.VMEM), gradient, old, *squares, old_acc, accumulator)


def per_device(pooled_grad, segment_map, unique_rows, live_counts, embedding, accumulator):
    columns = pooled_grad.shape[2]
    slots = unique_rows.shape[1]
    cols = lax.axis_size("col")
    half = slots // 2
    seg = jnp.transpose(segment_map, (1, 2, 0))
    seg = pltpu.with_memory_space_constraint(seg, pltpu.HBM)
    xt, ids, bound = prep(pooled_grad, seg)

    chips = [(z, y) for z in range(4) for y in range(4)]
    index = lambda z, y, c: ((z % 4) * 4 + y % 4) * 2 + c
    owner = ("z", "y", "core")

    def swap(a):
        return lax.ppermute(a, "core", [(0, 1), (1, 0)])

    def shift(a, first, by):
        move = lambda z, y, c: (z + by, y, c) if (c == 0) == first else (z, y + by, c)
        return lax.ppermute(a, owner, [(index(z, y, c), index(*move(z, y, c))) for z, y in chips for c in range(2)])

    run = lambda name, *jobs, **kw: sums(name, bound, ids, xt, half, jobs, **kw)
    both = (0, 1)
    sib = lambda step: (False, step, both, (None, None), False, BF)
    own = lambda step, parts, add, extra=None, split=True, kind=BF: (True, step, parts, (add, extra), split, kind)
    (sib_far,) = run("sib_far", sib(2))
    got_far = swap(sib_far)
    sib_next, sib_back = run("sib_next", sib(1), sib(3), after=(sib_far,))
    got_next, got_back = swap(sib_next), swap(sib_back)
    far_low, far_high = run("own_far", own(2, both, got_far), after=(sib_next,))
    low_got, high_got = shift(far_low, True, 1), shift(far_high, True, -1)
    next_high, back_low = run("free", own(1, (1,), got_next), own(3, (0,), got_back), after=(far_low,))
    next_high_got, back_low_got = shift(next_high, True, 1), shift(back_low, True, -1)
    next_low, back_high = run(
        "bound", own(1, (0,), got_next, low_got), own(3, (1,), got_back, high_got), after=(next_high,)
    )
    next_low_got, back_high_got = shift(next_low, True, 1), shift(back_high, True, -1)
    (sib_here,) = run("sib_here", sib(0), after=(next_low,))
    got_here = swap(sib_here)
    (here,) = run("own_here", own(0, both, None, None, False, F32), after=(sib_here,))
    gathered = gather(here, next_low_got, next_high_got, back_low_got, back_high_got)
    parts = list(fold(gathered, got_here))
    old, old_acc, table = old_values(unique_rows, embedding[0], accumulator, parts[1])
    for d in (3, 1, 2):
        parts[d] = shift(parts[d], False, d)
    mine, other = total(parts, old)
    gradient, squares = square(mine, swap(other))
    across = lambda a, k: lax.ppermute(a, "col", [(i, i ^ k) for i in range(cols)])
    pair = squares + across(squares, 1)
    squares = (pair, across(pair, 3))
    new_embedding, new_accumulator, _ = apply_rows(
        columns * cols, unique_rows, live_counts, table, gradient, old, squares, old_acc, accumulator
    )
    return (new_embedding[None], new_accumulator)


def solution(mesh):
    owner = ("z", "y", "core")
    split = Mesh(mesh.devices.reshape(4, 4, 2, mesh.devices.shape[1]), owner + ("col",))
    return jax.shard_map(
        per_device,
        mesh=split,
        in_specs=(
            P(owner, None, "col"),
            P(owner, None, None),
            P(owner, None),
            P(owner),
            P(owner, None, "col"),
            P(owner, None),
        ),
        out_specs=(P(owner, None, "col"), P(owner, None)),
        check_vma=False,
    )
```
